256 devices in a mesh: atm: 32 (over y, z_lo, core), ocn: 4 (over x), ch: 2 (over z_hi).
Axes of the slice: x: 4, y: 4, z: 8 (z_hi: 2, z_lo: 4; z = z_hi * 4 + z_lo), core: 2. Of those that a mesh axis runs over, the one named last changes fastest.
Arguments:
- atmosphere: bfloat16 [384, 1440, 384], P('atm', ('ocn', 'ch')), may hold values from -6 to 6
- ocean_state: bfloat16 [384, 1440, 200], P('atm', ('ocn', 'ch')), may hold values from -6 to 6
- surface_flux: float32 [4, 384, 1440], P(None, 'atm', ('ocn', 'ch')), may hold values from -6 to 6
- land_sea: int32 [384, 1440], P('atm', ('ocn', 'ch')), may hold values 0 or 1
- surface_read: bfloat16 [200], replicated, may hold values from -0.4375 to 0.4375
- surface_gain: float32 [384], replicated, may hold values from -4 to 4
- legendre: bfloat16 [384, 384, 384], P('atm'), may hold values from -0.3125 to 0.3125
- spectral_gain: float32 [384, 384], P(None, ('ocn', 'ch')), may hold values from -4 to 4
- mixing: bfloat16 [384, 384], replicated, may hold values from -0.3125 to 0.3125
- flux_weight: bfloat16 [384, 4], replicated, may hold values from -0.3125 to 0.3125
- flux_embed: float32 [4, 200], replicated, may hold values from -3 to 3
- conv_kernel: float32 [7, 7, 200], replicated, may hold values from -0.875 to 0.875
- norm_gain: float32 [200], replicated, may hold values from 0.25 to 1.75
- ocean_up: bfloat16 [200, 800], replicated, may hold values from -0.4375 to 0.4375
- ocean_down: bfloat16 [800, 200], replicated, may hold values from -0.21875 to 0.21875
Outputs:
- atmosphere_next: bfloat16 [384, 1440, 384], P('atm', ('ocn', 'ch'))
- flux_next: float32 [4, 384, 1440], P(None, 'atm', ('ocn', 'ch'))
- ocean_next: bfloat16 [384, 1440, 200], P('atm', ('ocn', 'ch'))
The draws below stay inside these ranges and needn't reach their ends.
All inputs are finite; a program needn't handle non-finite values. No bound on the sum of `land_sea` on one device may be relied on, other than what follows from the above.
Results may differ from the reference program's by a relative error of at most 0.009.
Values may be sent and summed in bfloat16 or wider, within the bound.
A program may use at most 128 MiB of HBM per device.

```python
import math
import jax
import jax.numpy as jnp
from jax import lax

C = 384
NLON = 1440
M = 384
L = 384
OC = 200
FC = 4
NLAT = 384
HID = 800


def set_ends(values, stream_key, smallest, top_value):
    place = [jax.random.randint(jax.random.fold_in(stream_key, axis), (), 0, length) for axis, length in enumerate(values.shape)]
    main_axis = values.shape.index(max(values.shape))
    next_to = place[:main_axis] + [(place[main_axis] + 1) % values.shape[main_axis]] + place[main_axis + 1:]
    return values.at[tuple(place)].set(smallest).at[tuple(next_to)].set(top_value)


def shard_levels(key, dims, pieces, least, top_value):
    gain = 1.0
    for axis_at, blocks in pieces:
        draws = jax.random.uniform(jax.random.fold_in(jax.random.fold_in(key, 6), axis_at), (blocks,), jnp.float32, least / len(pieces), top_value / len(pieces))
        gain = gain * jnp.repeat(jnp.exp(draws), dims[axis_at] // blocks).reshape((-1,) + (1,) * (len(dims) - 1 - axis_at))
    return gain


def gaussian(key, dims, spread, limit, split=(), held_as=jnp.bfloat16):
    drawn = jax.random.normal(key, dims, jnp.float32) * spread
    if len(split) > 0:
        drawn = shard_levels(key, dims, split, -0.22, 0.18) * drawn
    return jnp.clip(drawn, min=-limit, max=limit).astype(held_as)


def setup_inputs(seed: int = 0) -> dict:
    arg_keys = jax.random.split(jax.random.key(seed), 16)
    return {
        "atmosphere": gaussian(arg_keys[0], (NLAT, NLON, C), 1.0, 6.0, ((0, 32), (1, 8))),
        "ocean_state": gaussian(arg_keys[1], (NLAT, NLON, OC), 1.0, 6.0, ((0, 32), (1, 8))),
        "surface_flux": gaussian(arg_keys[2], (FC, NLAT, NLON), 1.0, 6.0, ((1, 32), (2, 8)), jnp.float32),
        "land_sea": set_ends((jax.random.randint(arg_keys[3], (NLAT, NLON), 0, 10) < 7).astype(jnp.int32), jax.random.fold_in(arg_keys[3], 1), 0, 1),
        "surface_read": gaussian(arg_keys[4], (OC,), OC ** -0.5, 0.4375),
        "surface_gain": gaussian(arg_keys[5], (C,), 1.0, 4.0, (), jnp.float32),
        "legendre": gaussian(arg_keys[6], (M, L, NLAT), NLAT ** -0.5, 0.3125, ((0, 32),)),
        "spectral_gain": gaussian(arg_keys[7], (L, C), 1.0, 4.0, ((1, 8),), jnp.float32),
        "mixing": gaussian(arg_keys[8], (C, C), C ** -0.5, 0.3125),
        "flux_weight": gaussian(arg_keys[9], (C, FC), C ** -0.5, 0.3125),
        "flux_embed": gaussian(arg_keys[10], (FC, OC), FC ** -0.5, 3.0, (), jnp.float32),
        "conv_kernel": gaussian(arg_keys[11], (7, 7, OC), 49 ** -0.5, 0.875, (), jnp.float32),
        "norm_gain": jnp.clip(1.0 + 0.15 * jax.random.normal(arg_keys[12], (OC,), jnp.float32), 0.25, 1.75),
        "ocean_up": gaussian(arg_keys[13], (OC, HID), OC ** -0.5, 0.4375),
        "ocean_down": gaussian(arg_keys[14], (HID, OC), HID ** -0.5, 0.21875),
    }


def lon_table(start, count, nlon, modes):
    lon = start + lax.iota(jnp.int32, count)
    wave = lax.iota(jnp.int32, modes)
    phase = lon[:, None] * wave[None, :] % nlon
    angle = phase.astype(jnp.float32) * (2.0 * math.pi / nlon)
    table = jnp.stack([jnp.cos(angle), -jnp.sin(angle)], axis=2) * nlon ** (-0.5)
    return table.reshape(count, 2 * modes).astype(jnp.bfloat16)

def depthwise(padded, kernel, rows, cols):
    total = jnp.zeros((rows, cols, padded.shape[2]), jnp.float32)
    for i in range(7):
        for j in range(7):
            total = total + kernel[i, j] * padded[i:i + rows, j:j + cols].astype(jnp.float32)
    return total

def reference(atmosphere, ocean_state, surface_flux, land_sea, surface_read, surface_gain, legendre, spectral_gain, mixing, flux_weight, flux_embed, conv_kernel, norm_gain, ocean_up, ocean_down):
    f32 = jnp.float32
    bf16 = jnp.bfloat16
    surface = jnp.einsum('alo,o->al', ocean_state.astype(f32), surface_read.astype(f32))
    forced = (atmosphere.astype(f32) + surface[:, :, None] * surface_gain).astype(bf16)
    table = lon_table(0, NLON, NLON, M)
    spectrum = jnp.einsum('alc,lk->ack', forced.astype(f32), table.astype(f32)).astype(bf16)
    blocks = spectrum.reshape(NLAT, C, M, 2).transpose(2, 0, 1, 3)

    def per_mode(item):
        plane, block = item
        coeffs = jnp.einsum('da,acp->pdc', plane.astype(f32), block.astype(f32))
        filtered = (coeffs * spectral_gain[None]).astype(bf16)
        return jnp.einsum('da,pdc->acp', plane.astype(f32), filtered.astype(f32)).astype(bf16)
    synth = lax.map(per_mode, (legendre, blocks))
    synth = synth.transpose(1, 2, 0, 3).reshape(NLAT, C, 2 * M)
    grid = jnp.einsum('ack,lk->alc', synth.astype(f32), table.astype(f32)).astype(bf16)
    mixed_in = forced.astype(f32) + grid.astype(f32)
    active = jax.nn.gelu(mixed_in).astype(bf16)
    atmosphere_next = (mixed_in + jnp.einsum('alc,cd->ald', active.astype(f32), mixing.astype(f32))).astype(bf16)
    flux_next = jnp.einsum('alc,cf->fal', atmosphere_next.astype(f32), flux_weight.astype(f32))
    embed = jnp.einsum('fal,fo->alo', surface_flux, flux_embed, precision=lax.Precision.HIGHEST)
    driven = (ocean_state.astype(f32) + embed).astype(bf16)
    padded = jnp.pad(driven, ((3, 3), (0, 0), (0, 0)))
    padded = jnp.concatenate([padded[:, -3:], padded, padded[:, :3]], axis=1)
    conv = depthwise(padded, conv_kernel, NLAT, NLON)
    mean = lax.optimization_barrier(jnp.mean(conv, axis=-1, keepdims=True))
    centred = conv - mean
    var = lax.optimization_barrier(jnp.mean(centred * centred, axis=-1, keepdims=True))
    normed = (centred * lax.rsqrt(var + 1e-05) * norm_gain).astype(bf16)
    hidden = jax.nn.gelu(jnp.einsum('alo,oh->alh', normed.astype(f32), ocean_up.astype(f32))).astype(bf16)
    update = jnp.einsum('alh,ho->alo', hidden.astype(f32), ocean_down.astype(f32))
    ocean_next = jnp.where(land_sea[:, :, None] == 1, driven.astype(f32) + update, jnp.zeros((), f32)).astype(bf16)
    return (atmosphere_next, flux_next, ocean_next)
```

```python
import math

import jax
import jax.numpy as jnp
import ml_dtypes
import numpy as np
from jax import lax
from jax.experimental import pallas as pl
from jax.experimental.pallas import tpu as pltpu
from jax.sharding import PartitionSpec as P

M = 384
NLON = 1440
C = 384
OC = 200
HID = 800
LATS = 12
LONS = 180
ROWS = 192
CB = 48
PEERS = 32
MODES = 24
CHUNKS = ((0, 8, 384), (8, 4, 256))
MESH = pl.DeviceIdType.MESH
F32 = jnp.float32
BF16 = jnp.bfloat16
VMEM_LIMIT = 60 * 2**20


def lon_tables():
    lon = np.arange(NLON, dtype=np.int64)
    wave = np.arange(M, dtype=np.int64)
    phase = (lon[:, None] * wave[None, :]) % NLON
    angle = phase.astype(np.float32) * np.float32(2.0 * math.pi / NLON)
    table = np.stack([np.cos(angle), -np.sin(angle)], axis=2) * np.float32(NLON**-0.5)
    table = table.astype(np.float32).reshape(4, 2, LONS, 2 * M).transpose(1, 0, 2, 3)
    padded = np.zeros((2, 4, ROWS, 2 * M), np.float32)
    padded[:, :, :LONS] = table
    inverse = padded.reshape(2, 4 * ROWS, 2 * M).astype(ml_dtypes.bfloat16)
    return np.ascontiguousarray(inverse.transpose(0, 2, 1)), inverse


def segments(src, dst, count):
    out = []
    done = 0
    while done < count:
        s, d = src + done, dst + done
        step = min(count - done, 128 - s % 128, 128 - d % 128)
        out.append((s // 128, d // 128, (d - s) % 128, d % 128, d % 128 + step))
        done += step
    return out


def move_lanes(moves, tiles, get, rows):
    lane = lax.broadcasted_iota(jnp.int32, (rows, 128), 1)
    out = [None] * tiles
    for key, src, dst, count in moves:
        for s_tile, d_tile, shift, low, high in segments(src, dst, count):
            piece = get(key, s_tile)
            if shift:
                piece = pltpu.roll(piece, shift, axis=1)
            if out[d_tile] is None:
                if low == 0:
                    out[d_tile] = jnp.where(lane < high, piece, 0.0)
                else:
                    out[d_tile] = jnp.where((lane >= low) & (lane < high), piece, 0.0)
            else:
                out[d_tile] = jnp.where((lane >= low) & (lane < high), piece, out[d_tile])
    return out


def body(
    atm_ref, oc_ref, flux_ref, land_ref, read_ref, gain_ref, leg_hbm, sgain_ref, mix_ref, fw_ref,
    embed_ref, ck_ref, ngain_ref, up_ref, down_ref, tf_hbm, ti_hbm,
    atm_out, flux_out, oc_out,
    tf, ti, leg, leg_p, leg_t, forced,
    pack_a, pack_b, got_a, got_b, spec_a, spec_b, rspec_a, rspec_b, rsum, ssum,
    syn_a, syn_b, rsyn_a, rsyn_b, sy_a, sy_b, gs_a, gs_b, rg_a, rg_b,
    sg2, cols, colt, fws, drv, edge_l, edge_r, halo_l, halo_r, cpad, cker,
    in_sem, x_send, x_recv, z_send, z_recv, zi_send, zi_recv, xi_send, xi_recv, h_send, h_recv, loc_sem,
):
    pack, got, spec, rspec = (pack_a, pack_b), (got_a, got_b), (spec_a, spec_b), (rspec_a, rspec_b)
    syn, rsyn, sy, gs, rg = (syn_a, syn_b), (rsyn_a, rsyn_b), (sy_a, sy_b), (gs_a, gs_b), (rg_a, rg_b)
    a_id = lax.axis_index("atm")
    x = lax.axis_index("ocn")
    h = lax.axis_index("ch")
    core = lax.rem(a_id, 2)
    yz = a_id // 2
    y0 = yz // 4
    z0 = lax.rem(yz, 4)
    me = 2 * x + core
    lon_block = 2 * x + h
    self_peer = core == h
    n_remote = PEERS - self_peer.astype(jnp.int32)

    tf_copy = pltpu.make_async_copy(tf_hbm.at[h], tf, in_sem.at[0])
    ti_copy = pltpu.make_async_copy(ti_hbm.at[h], ti, in_sem.at[1])
    leg_copy = pltpu.make_async_copy(leg_hbm, leg, in_sem.at[2])
    tf_copy.start()
    leg_copy.start()
    ti_copy.start()

    def row_dev(q):
        return {"atm": 2 * yz + lax.rem(q, 2), "ocn": q // 2, "ch": h}

    def mode_dev(j):
        return {"atm": j, "ocn": x, "ch": core}

    def band_dev(j):
        return {"atm": (j // 2) * 2 + h, "ocn": x, "ch": lax.rem(j, 2)}

    def lat_dev(step):
        return {"atm": lax.rem(a_id + step + 32, 32), "ocn": x, "ch": h}

    def lon_dev(step):
        b = lax.rem(lon_block + step + 8, 8)
        return {"atm": a_id, "ocn": b // 2, "ch": lax.rem(b, 2)}

    barrier = pltpu.get_barrier_semaphore()

    def greet(device):
        pl.semaphore_signal(barrier, inc=1, device_id=device, device_id_type=MESH)

    def greet_row(i, carry):
        greet(row_dev(lax.rem(me + i, 8)))
        return carry

    lax.fori_loop(1, 8, greet_row, 0)
    for step in (-1, 1):
        greet(lat_dev(step))
        greet(lon_dev(step))

    def greet_peers(j, carry):
        @pl.when(jnp.logical_not(self_peer & (j == a_id)))
        def _():
            greet(mode_dev(j))

        @pl.when(jnp.logical_not(self_peer & (j == 2 * yz + h)))
        def _():
            greet(band_dev(j))

        return carry

    lax.fori_loop(0, PEERS, greet_peers, 0)

    forced[:, 176:192, :] = jnp.zeros((LATS, 16, C), BF16)

    def force(a, carry):
        seen = oc_ref[a].astype(F32) * read_ref[...].astype(F32)
        surface = jnp.sum(seen, axis=1, keepdims=True)
        forced[a, 0:LONS, :] = (atm_ref[a].astype(F32) + surface * gain_ref[...]).astype(BF16)
        return carry

    lax.fori_loop(0, LATS, force, 0)

    def pack_chunk(k):
        a0, na, width = CHUNKS[k]

        def rows_step(rb, carry):
            r0 = pl.multiple_of(rb * 48, 16)
            held = {}
            for a in range(na):
                for t in range(3):
                    held[a, t] = forced[a0 + a, pl.ds(r0, 48), 128 * t : 128 * t + 128].astype(F32)
            for q in range(8):
                moves = [(a, CB * q, CB * a, CB) for a in range(na)]
                tiles = move_lanes(moves, width // 128, lambda key, t: held[key, t], 48)
                for t, value in enumerate(tiles):
                    pack[k][q, pl.ds(r0, 48), 128 * t : 128 * t + 128] = value.astype(BF16)
            return carry

        lax.fori_loop(0, 4, rows_step, 0)

    def x_copy(k, q):
        return pltpu.make_async_remote_copy(
            src_ref=pack[k].at[q], dst_ref=got[k].at[core, x], send_sem=x_send.at[k],
            recv_sem=x_recv.at[k], device_id=row_dev(q), device_id_type=MESH,
        )

    def x_start(k):
        pltpu.make_async_copy(pack[k].at[me], got[k].at[core, x], loc_sem.at[k]).start()

        def go(i, carry):
            x_copy(k, lax.rem(me + i, 8)).start()
            return carry

        lax.fori_loop(1, 8, go, 0)

    def covers(ref, send, recv):
        return pltpu.make_async_remote_copy(
            src_ref=ref, dst_ref=ref, send_sem=send, recv_sem=recv,
            device_id=lat_dev(1), device_id_type=MESH,
        )

    def x_all(k, send, recv):
        return covers(pack[k].at[pl.ds(0, 7)], send.at[k], recv.at[k])

    def x_wait(k):
        pltpu.make_async_copy(pack[k].at[me], got[k].at[core, x], loc_sem.at[k]).wait()
        x_all(k, x_send, x_recv).wait_recv()

    pack_chunk(1)
    pl.semaphore_wait(barrier, 2 * n_remote + 7 + 4)
    x_start(1)
    pack_chunk(0)
    x_start(0)

    cols[...] = jnp.zeros_like(cols)
    for f in range(4):
        cols[16 * f : 16 * f + LATS, 0:LONS] = flux_ref[f]
    cols[64 : 64 + LATS, 0:LONS] = land_ref[...].astype(F32)
    colt[...] = jnp.transpose(cols[...], (1, 0))
    drv[3:15, 176:192, :] = jnp.zeros((LATS, 16, 256), BF16)
    drv[3:15, :, 128:256] = jnp.zeros((LATS, ROWS, 128), BF16)
    for a in range(LATS):
        total = oc_ref[a].astype(F32)
        for f in range(4):
            total = total + colt[0:LONS, 16 * f + a : 16 * f + a + 1] * embed_ref[f : f + 1, :]
        drv[a + 3, 0:LONS, 0:OC] = total.astype(BF16)

    lat_low = pltpu.make_async_remote_copy(
        src_ref=drv.at[pl.ds(12, 3)], dst_ref=drv.at[pl.ds(0, 3)], send_sem=h_send.at[0],
        recv_sem=h_recv.at[0], device_id=lat_dev(1), device_id_type=MESH,
    )
    lat_high = pltpu.make_async_remote_copy(
        src_ref=drv.at[pl.ds(3, 3)], dst_ref=drv.at[pl.ds(15, 3)], send_sem=h_send.at[1],
        recv_sem=h_recv.at[1], device_id=lat_dev(-1), device_id_type=MESH,
    )
    lat_low.start()
    lat_high.start()

    sg2[...] = jnp.zeros_like(sg2)
    sg2[:, 0:CB] = sgain_ref[...]
    sg2[...] = sg2[...] + pltpu.roll(sg2[...], CB, axis=1)
    fws[...] = jnp.zeros_like(fws)
    fws[:, 0:4] = fw_ref[...].astype(F32)
    fwt = jnp.transpose(fws[...], (1, 0))[0:16].astype(BF16)
    cker[...] = jnp.zeros_like(cker)
    for i in range(7):
        cker[8 * i : 8 * i + 7, 0:OC] = ck_ref[i]

    leg_copy.wait()
    new = lax.broadcasted_iota(jnp.int32, (C, C), 0)
    old = lax.broadcasted_iota(jnp.int32, (C, C), 1)
    order = (old == lax.rem(new, 32) * LATS + new // 32).astype(F32).astype(BF16)

    def permute(m, carry):
        table = leg[m]
        leg_p[m] = lax.dot_general(
            table, order, (((1,), (1,)), ((), ())), preferred_element_type=F32
        ).astype(BF16)
        leg_t[m] = lax.dot_general(
            order, table, (((1,), (1,)), ((), ())), preferred_element_type=F32
        ).astype(BF16)
        return carry

    lax.fori_loop(0, LATS, permute, 0)

    slot = 2 * yz + h

    def z_copy(k, j):
        return pltpu.make_async_remote_copy(
            src_ref=spec[k].at[j], dst_ref=rspec[k].at[slot], send_sem=z_send.at[k],
            recv_sem=z_recv.at[k], device_id=mode_dev(j), device_id_type=MESH,
        )

    def z_local(k):
        return pltpu.make_async_copy(spec[k].at[a_id], rspec[k].at[slot], loc_sem.at[2 + k])

    def forward(k):
        width = CHUNKS[k][2]

        def step(i, carry):
            yb = lax.rem(y0 + i, 4)
            lhs = tf[pl.ds(pl.multiple_of(yb * 192, 16), 192), :]
            halves = [
                jnp.dot(lhs, got[k][s].reshape(4 * ROWS, width), preferred_element_type=F32)
                for s in range(2)
            ]
            for n in range(8):
                part = slice(MODES * n, MODES * n + MODES)
                both = jnp.concatenate([halves[0][part], halves[1][part]], axis=0)
                spec[k][yb * 8 + n] = both.astype(BF16)

            def send(n, c2):
                j = yb * 8 + lax.rem(2 * z0 + n, 8)
                mine = self_peer & (j == a_id)

                @pl.when(jnp.logical_not(mine))
                def _():
                    z_copy(k, j).start()

                @pl.when(mine)
                def _():
                    z_local(k).start()

                return c2

            lax.fori_loop(0, 8, send, 0)
            return carry

        lax.fori_loop(0, 4, step, 0)

    def peers_all(k, send, recv, act):
        @pl.when(self_peer)
        def _():
            act(covers(rspec[k].at[pl.ds(0, PEERS - 1)], send.at[k], recv.at[k]))

        @pl.when(jnp.logical_not(self_peer))
        def _():
            act(covers(rspec[k], send.at[k], recv.at[k]))

    tf_copy.wait()
    x_wait(1)
    forward(1)

    lat_low.wait_recv()
    lat_high.wait_recv()

    @pl.when(a_id == 0)
    def _():
        drv[0:3] = jnp.zeros((3, ROWS, 256), BF16)

    @pl.when(a_id == 31)
    def _():
        drv[15:18] = jnp.zeros((3, ROWS, 256), BF16)

    edge_l[...] = drv[:, 0:16, :]
    edge_r[...] = drv[:, 176:192, :]
    lon_low = pltpu.make_async_remote_copy(
        src_ref=edge_r, dst_ref=halo_l, send_sem=h_send.at[2],
        recv_sem=h_recv.at[2], device_id=lon_dev(1), device_id_type=MESH,
    )
    lon_high = pltpu.make_async_remote_copy(
        src_ref=edge_l, dst_ref=halo_r, send_sem=h_send.at[3],
        recv_sem=h_recv.at[3], device_id=lon_dev(-1), device_id_type=MESH,
    )
    lon_low.start()
    lon_high.start()

    x_wait(0)
    forward(0)

    lon_low.wait_recv()
    lon_high.wait_recv()

    def place(r, carry):
        cpad[r, 0:8, :] = pltpu.roll(halo_l[r].astype(F32), 15, axis=0)[0:8]
        cpad[r, 176:192, :] = jnp.zeros((16, 256), F32)
        cpad[r, 183:189, :] = halo_r[r].astype(F32)[0:6]
        cpad[r, 3:183, :] = drv[r, 0:LONS, :].astype(F32)
        return carry

    lax.fori_loop(0, LATS + 6, place, 0)
    lane = lax.broadcasted_iota(jnp.int32, (ROWS, 256), 1)

    def ocean(a, carry):
        halves = []
        for t in range(2):
            part = slice(128 * t, 128 * t + 128)
            total = None
            for j in range(7):
                acc = None
                for i in range(7):
                    term = cker[8 * i + j : 8 * i + j + 1, part] * cpad[a + i, :, part]
                    acc = term if acc is None else acc + term
                if j:
                    acc = pltpu.roll(acc, ROWS - j, axis=0)
                total = acc if total is None else total + acc
            halves.append(total)
        conv = jnp.concatenate(halves, axis=1)
        mean = jnp.sum(conv, axis=1, keepdims=True) * (1.0 / OC)
        centred = jnp.where(lane < OC, conv - mean, 0.0)
        var = jnp.sum(centred * centred, axis=1, keepdims=True) * (1.0 / OC)
        scaled = centred * lax.rsqrt(var + 1e-05)
        normed = (scaled[:, 0:OC] * ngain_ref[...]).astype(BF16)
        hidden = jax.nn.gelu(
            jnp.dot(normed, up_ref[...], preferred_element_type=F32)
        ).astype(BF16)
        update = jnp.dot(hidden, down_ref[...], preferred_element_type=F32)
        mask_lane = lax.broadcasted_iota(jnp.int32, (ROWS, 128), 1)
        sea = jnp.sum(
            jnp.where(mask_lane == 64 + a, colt[0:ROWS, :], 0.0), axis=1, keepdims=True
        )
        held = drv[a + 3, :, 0:OC].astype(F32) + update
        oc_out[a] = jnp.where(sea == 1.0, held, 0.0)[0:LONS].astype(BF16)
        return carry

    lax.fori_loop(0, LATS, ocean, 0)

    def add_halves(k):
        first = CHUNKS[k][0] * CB // 128

        def step(i, carry):
            both = rspec[k][2 * i].astype(F32) + rspec[k][2 * i + 1].astype(F32)
            for t in range(CHUNKS[k][2] // 128):
                rsum[first + t, pl.ds(pl.multiple_of(i * 48, 8), 48), :] = both[
                    :, 128 * t : 128 * t + 128
                ]
            return carry

        lax.fori_loop(0, 16, step, 0)

    def z_wait(k):
        peers_all(k, z_send, z_recv, lambda copy: copy.wait_recv())

        @pl.when(self_peer)
        def _():
            z_local(k).wait()

    z_wait(1)
    add_halves(1)
    z_wait(0)
    add_halves(0)
    lane32 = lax.broadcasted_iota(jnp.int32, (32, 128), 1)

    def legendre_step(m, carry):
        planes = []
        for p in range(2):
            rows = [
                rsum[t, pl.ds(2 * m + p, 32, stride=MODES), :]
                for t in range(5)
            ]
            planes.append(rows)
        blocks = []
        for a in range(LATS):
            moves = [(p, CB * a, CB * p, CB) for p in range(2)]
            blocks.append(move_lanes(moves, 1, lambda key, t: planes[key][t], 32)[0])
        spectrum = jnp.concatenate(blocks, axis=0).astype(BF16)
        coeffs = jnp.dot(leg_p[m], spectrum, preferred_element_type=F32)
        filtered = (coeffs * sg2[...]).astype(BF16)
        synth = jnp.dot(leg_t[m], filtered, preferred_element_type=F32)
        for p in range(2):
            moves = [(a, CB * p, CB * a, CB) for a in range(LATS)]
            tiles = move_lanes(moves, 5, lambda key, t: synth[32 * key : 32 * key + 32], 32)
            for t, value in enumerate(tiles):
                ssum[t, pl.ds(2 * m + p, 32, stride=MODES), :] = value
        return carry

    lax.fori_loop(0, LATS, legendre_step, 0)

    def zi_copy(k, j):
        return pltpu.make_async_remote_copy(
            src_ref=syn[k].at[j // 2], dst_ref=rsyn[k].at[a_id], send_sem=zi_send.at[k],
            recv_sem=zi_recv.at[k], device_id=band_dev(j), device_id_type=MESH,
        )

    def zi_local(k):
        return pltpu.make_async_copy(syn[k].at[yz], rsyn[k].at[a_id], loc_sem.at[4 + k])

    def back(k):
        first = CHUNKS[k][0] * CB // 128

        def step(i, carry):
            b = lax.rem(y0 + i // 4, 4) * 4 + lax.rem(z0 + i, 4)
            for t in range(CHUNKS[k][2] // 128):
                syn[k][b, :, 128 * t : 128 * t + 128] = ssum[
                    first + t, pl.ds(pl.multiple_of(b * 48, 8), 48), :
                ].astype(BF16)
            for n in range(2):
                j = 2 * b + n
                mine = self_peer & (j == 2 * yz + h)

                @pl.when(jnp.logical_not(mine))
                def _():
                    zi_copy(k, j).start()

                @pl.when(mine)
                def _():
                    zi_local(k).start()

            return carry

        lax.fori_loop(0, 16, step, 0)

    back(0)
    back(1)

    def zi_wait(k):
        peers_all(k, zi_send, zi_recv, lambda copy: copy.wait_recv())

        @pl.when(self_peer)
        def _():
            zi_local(k).wait()

    def xi_copy(k, q):
        return pltpu.make_async_remote_copy(
            src_ref=gs[k].at[q], dst_ref=rg[k].at[me], send_sem=xi_send.at[k],
            recv_sem=xi_recv.at[k], device_id=row_dev(q), device_id_type=MESH,
        )

    def xi_local(k):
        return pltpu.make_async_copy(gs[k].at[me], rg[k].at[me], loc_sem.at[6 + k])

    def inverse(k):
        def regroup(i, carry):
            first = rsyn[k][2 * i].astype(F32)
            second = rsyn[k][2 * i + 1].astype(F32)
            for s in range(2):
                part = slice(MODES * s, MODES * s + MODES)
                both = jnp.concatenate([first[part], second[part]], axis=0)
                sy[k][s, pl.ds(pl.multiple_of(i * 48, 16), 48), :] = both.astype(BF16)
            return carry

        lax.fori_loop(0, 16, regroup, 0)

        def step(i, carry):
            xb = lax.rem(x + i, 4)
            lhs = ti[pl.ds(pl.multiple_of(xb * ROWS, 16), ROWS), :]
            for s in range(2):
                q = 2 * xb + s
                gs[k][q] = jnp.dot(lhs, sy[k][s], preferred_element_type=F32).astype(BF16)

                @pl.when(q != me)
                def _():
                    xi_copy(k, q).start()

                @pl.when(q == me)
                def _():
                    xi_local(k).start()

            return carry

        lax.fori_loop(0, 4, step, 0)

    def xi_wait(k):
        x_all(k, xi_send, xi_recv).wait_recv()
        xi_local(k).wait()

    def finish(k):
        a0, na, width = CHUNKS[k]
        for a in range(na):
            moves = [(q, CB * a, CB * q, CB) for q in range(8)]
            tiles = move_lanes(
                moves, 3,
                lambda key, t: rg[k][key, :, 128 * t : 128 * t + 128].astype(F32), ROWS,
            )
            grid = jnp.concatenate(tiles, axis=1)
            mixed = forced[a0 + a].astype(F32) + grid
            active = jax.nn.gelu(mixed).astype(BF16)
            result = mixed + jnp.dot(active, mix_ref[...], preferred_element_type=F32)
            result = result.astype(BF16)
            atm_out[a0 + a] = result[0:LONS]
            fluxes = lax.dot_general(
                fwt, result, (((1,), (1,)), ((), ())), preferred_element_type=F32
            )
            for f in range(4):
                flux_out[f, a0 + a : a0 + a + 1, :] = fluxes[f : f + 1, 0:LONS]

    ti_copy.wait()
    zi_wait(0)
    inverse(0)
    xi_wait(0)
    finish(0)
    zi_wait(1)
    inverse(1)
    xi_wait(1)
    finish(1)

    for k in range(2):
        x_all(k, x_send, x_recv).wait_send()
        x_all(k, xi_send, xi_recv).wait_send()
        peers_all(k, z_send, z_recv, lambda copy: copy.wait_send())
        peers_all(k, zi_send, zi_recv, lambda copy: copy.wait_send())
    for copy in (lat_low, lat_high, lon_low, lon_high):
        copy.wait_send()


def local(
    atmosphere, ocean_state, surface_flux, land_sea, surface_read, surface_gain, legendre,
    spectral_gain, mixing, flux_weight, flux_embed, conv_kernel, norm_gain, ocean_up, ocean_down,
):
    forward_table, inverse_table = lon_tables()
    vm = pl.BlockSpec(memory_space=pltpu.VMEM)
    hbm = pl.BlockSpec(memory_space=pl.ANY)
    wide = [w for _, _, w in CHUNKS]

    def pair(*dims):
        return [pltpu.VMEM(dims + (w,), BF16) for w in wide]

    dma = pltpu.SemaphoreType.DMA
    return pl.pallas_call(
        body,
        out_shape=(
            jax.ShapeDtypeStruct((LATS, LONS, C), BF16),
            jax.ShapeDtypeStruct((4, LATS, LONS), F32),
            jax.ShapeDtypeStruct((LATS, LONS, OC), BF16),
        ),
        in_specs=[vm] * 6 + [hbm] + [vm] * 8 + [hbm] * 2,
        out_specs=(vm, vm, vm),
        scratch_shapes=[
            pltpu.VMEM((2 * M, 4 * ROWS), BF16),
            pltpu.VMEM((4 * ROWS, 2 * M), BF16),
            pltpu.VMEM((LATS, C, C), BF16),
            pltpu.VMEM((LATS, C, C), BF16),
            pltpu.VMEM((LATS, C, C), BF16),
            pltpu.VMEM((LATS, ROWS, C), BF16),
            *pair(8, ROWS),
            *pair(2, 4, ROWS),
            *pair(PEERS, 48),
            *pair(PEERS, 48),
            pltpu.VMEM((5, 768, 128), F32),
            pltpu.VMEM((5, 768, 128), F32),
            *pair(16, 48),
            *pair(PEERS, 48),
            *pair(2, 768),
            *pair(8, ROWS),
            *pair(8, ROWS),
            pltpu.VMEM((C, 128), F32),
            pltpu.VMEM((128, 256), F32),
            pltpu.VMEM((256, 128), F32),
            pltpu.VMEM((C, 128), F32),
            pltpu.VMEM((LATS + 6, ROWS, 256), BF16),
            pltpu.VMEM((LATS + 6, 16, 256), BF16),
            pltpu.VMEM((LATS + 6, 16, 256), BF16),
            pltpu.VMEM((LATS + 6, 16, 256), BF16),
            pltpu.VMEM((LATS + 6, 16, 256), BF16),
            pltpu.VMEM((LATS + 6, ROWS, 256), F32),
            pltpu.VMEM((56, 256), F32),
            dma((3,)), dma((2,)), dma((2,)), dma((2,)), dma((2,)), dma((2,)), dma((2,)),
            dma((2,)), dma((2,)), dma((4,)), dma((4,)), dma((8,)),
        ],
        compiler_params=pltpu.CompilerParams(
            collective_id=0, has_side_effects=True, vmem_limit_bytes=VMEM_LIMIT
        ),
        name="window",
    )(
        atmosphere, ocean_state, surface_flux, land_sea, surface_read.reshape(1, OC),
        surface_gain.reshape(1, C), legendre, spectral_gain, mixing, flux_weight, flux_embed,
        conv_kernel, norm_gain.reshape(1, OC), ocean_up, ocean_down,
        jnp.asarray(forward_table), jnp.asarray(inverse_table),
    )


def solution(mesh):
    grid = P("atm", ("ocn", "ch"), None)
    return jax.shard_map(
        local,
        mesh=mesh,
        in_specs=(
            grid, grid, P(None, "atm", ("ocn", "ch")), P("atm", ("ocn", "ch")), P(), P(),
            P("atm", None, None), P(None, ("ocn", "ch")), P(), P(), P(), P(), P(), P(), P(),
        ),
        out_specs=(grid, P(None, "atm", ("ocn", "ch")), grid),
        check_vma=False,
    )
```

```python
import math

import jax
import jax.numpy as jnp
import ml_dtypes
import numpy as np
from jax import lax
from jax.experimental import pallas as pl
from jax.experimental.pallas import tpu as pltpu
from jax.sharding import PartitionSpec as P

M = 384
NLON = 1440
C = 384
OC = 200
HID = 800
LATS = 12
LONS = 180
ROWS = 192
CB = 48
PEERS = 32
MODES = 24
CHUNKS = ((0, 8, 384), (8, 4, 256))
MESH = pl.DeviceIdType.MESH
F32 = jnp.float32
BF16 = jnp.bfloat16
VMEM_LIMIT = 60 * 2**20


def lon_tables():
    lon = np.arange(NLON, dtype=np.int64)
    wave = np.arange(M, dtype=np.int64)
    phase = (lon[:, None] * wave[None, :]) % NLON
    angle = phase.astype(np.float32) * np.float32(2.0 * math.pi / NLON)
    table = np.stack([np.cos(angle), -np.sin(angle)], axis=2) * np.float32(NLON**-0.5)
    table = table.astype(np.float32).reshape(4, 2, LONS, 2 * M).transpose(1, 0, 2, 3)
    padded = np.zeros((2, 4, ROWS, 2 * M), np.float32)
    padded[:, :, :LONS] = table
    inverse = padded.reshape(2, 4 * ROWS, 2 * M).astype(ml_dtypes.bfloat16)
    return np.ascontiguousarray(inverse.transpose(0, 2, 1)), inverse


def segments(src, dst, count):
    out = []
    done = 0
    while done < count:
        s, d = src + done, dst + done
        step = min(count - done, 128 - s % 128, 128 - d % 128)
        out.append((s // 128, d // 128, (d - s) % 128, d % 128, d % 128 + step))
        done += step
    return out


def move_lanes(moves, tiles, get, rows):
    lane = lax.broadcasted_iota(jnp.int32, (rows, 128), 1)
    out = [None] * tiles
    for key, src, dst, count in moves:
        for s_tile, d_tile, shift, low, high in segments(src, dst, count):
            piece = get(key, s_tile)
            if shift:
                piece = pltpu.roll(piece, shift, axis=1)
            if out[d_tile] is None:
                if low == 0:
                    out[d_tile] = jnp.where(lane < high, piece, 0.0)
                else:
                    out[d_tile] = jnp.where((lane >= low) & (lane < high), piece, 0.0)
            else:
                out[d_tile] = jnp.where((lane >= low) & (lane < high), piece, out[d_tile])
    return out


def body(
    atm_ref, oc_ref, flux_ref, land_ref, read_ref, gain_ref, leg_hbm, sgain_ref, mix_ref, fw_ref,
    embed_ref, ck_ref, ngain_ref, up_ref, down_ref, tf_hbm, ti_hbm,
    atm_out, flux_out, oc_out,
    tf, ti, leg, leg_p, leg_t, forced,
    pack_a, pack_b, got_a, got_b, spec_a, spec_b, rspec_a, rspec_b, rsum, ssum,
    syn_a, syn_b, rsyn_a, rsyn_b, sy_a, sy_b, gs_a, gs_b, rg_a, rg_b,
    coef, filt, sgs, sg2, cols, colt, fws, drv, edge_l, edge_r, halo_l, halo_r, cpad, cker,
    in_sem, x_send, x_recv, z_send, z_recv, zi_send, zi_recv, xi_send, xi_recv, h_send, h_recv, loc_sem,
):
    pack, got, spec, rspec = (pack_a, pack_b), (got_a, got_b), (spec_a, spec_b), (rspec_a, rspec_b)
    syn, rsyn, sy, gs, rg = (syn_a, syn_b), (rsyn_a, rsyn_b), (sy_a, sy_b), (gs_a, gs_b), (rg_a, rg_b)
    a_id = lax.axis_index("atm")
    x = lax.axis_index("ocn")
    h = lax.axis_index("ch")
    core = lax.rem(a_id, 2)
    yz = a_id // 2
    y0 = yz // 4
    z0 = lax.rem(yz, 4)
    me = 2 * x + core
    lon_block = 2 * x + h
    self_peer = core == h
    n_remote = PEERS - self_peer.astype(jnp.int32)

    tf_copy = pltpu.make_async_copy(tf_hbm.at[h], tf, in_sem.at[0])
    ti_copy = pltpu.make_async_copy(ti_hbm.at[h], ti, in_sem.at[1])
    leg_copy = pltpu.make_async_copy(leg_hbm, leg, in_sem.at[2])
    tf_copy.start()
    leg_copy.start()
    ti_copy.start()

    def row_dev(q):
        return {"atm": 2 * yz + lax.rem(q, 2), "ocn": q // 2, "ch": h}

    def mode_dev(j):
        return {"atm": j, "ocn": x, "ch": core}

    def band_dev(j):
        return {"atm": (j // 2) * 2 + h, "ocn": x, "ch": lax.rem(j, 2)}

    def lat_dev(step):
        return {"atm": lax.rem(a_id + step + 32, 32), "ocn": x, "ch": h}

    def lon_dev(step):
        b = lax.rem(lon_block + step + 8, 8)
        return {"atm": a_id, "ocn": b // 2, "ch": lax.rem(b, 2)}

    barrier = pltpu.get_barrier_semaphore()

    def greet(device):
        pl.semaphore_signal(barrier, inc=1, device_id=device, device_id_type=MESH)

    def greet_row(i, carry):
        greet(row_dev(lax.rem(me + i, 8)))
        return carry

    lax.fori_loop(1, 8, greet_row, 0)
    for step in (-1, 1):
        greet(lat_dev(step))
        greet(lon_dev(step))

    def greet_peers(j, carry):
        @pl.when(jnp.logical_not(self_peer & (j == a_id)))
        def _():
            greet(mode_dev(j))

        @pl.when(jnp.logical_not(self_peer & (j == 2 * yz + h)))
        def _():
            greet(band_dev(j))

        return carry

    lax.fori_loop(0, PEERS, greet_peers, 0)

    forced[:, 176:192, :] = jnp.zeros((LATS, 16, C), BF16)

    read_row = read_ref[...].astype(F32).reshape(1, OC)

    def force(a, carry):
        seen = oc_ref[a].astype(F32) * read_row
        surface = jnp.sum(seen, axis=1, keepdims=True)
        for t in range(3):
            part = slice(128 * t, 128 * t + 128)
            total = atm_ref[a, :, part].astype(F32) + surface * gain_ref[t : t + 1, :]
            forced[a, 0:LONS, part] = total.astype(BF16)
        return carry

    lax.fori_loop(0, LATS, force, 0)

    def pack_chunk(k):
        a0, na, width = CHUNKS[k]

        def rows_step(rb, carry):
            r0 = pl.multiple_of(rb * 48, 16)
            held = {}
            for a in range(na):
                for t in range(3):
                    held[a, t] = forced[a0 + a, pl.ds(r0, 48), 128 * t : 128 * t + 128].astype(F32)
            for q in range(8):
                moves = [(a, CB * q, CB * a, CB) for a in range(na)]
                tiles = move_lanes(moves, width // 128, lambda key, t: held[key, t], 48)
                for t, value in enumerate(tiles):
                    pack[k][q, pl.ds(r0, 48), 128 * t : 128 * t + 128] = value.astype(BF16)
            return carry

        lax.fori_loop(0, 4, rows_step, 0)

    def x_copy(k, q):
        return pltpu.make_async_remote_copy(
            src_ref=pack[k].at[q], dst_ref=got[k].at[core, x], send_sem=x_send.at[k],
            recv_sem=x_recv.at[k], device_id=row_dev(q), device_id_type=MESH,
        )

    def x_start(k):
        pltpu.make_async_copy(pack[k].at[me], got[k].at[core, x], loc_sem.at[k]).start()

        def go(i, carry):
            x_copy(k, lax.rem(me + i, 8)).start()
            return carry

        lax.fori_loop(1, 8, go, 0)

    def covers(ref, send, recv):
        return pltpu.make_async_remote_copy(
            src_ref=ref, dst_ref=ref, send_sem=send, recv_sem=recv,
            device_id=lat_dev(1), device_id_type=MESH,
        )

    def x_all(k, send, recv):
        return covers(pack[k].at[pl.ds(0, 7)], send.at[k], recv.at[k])

    def x_wait(k):
        pltpu.make_async_copy(pack[k].at[me], got[k].at[core, x], loc_sem.at[k]).wait()
        x_all(k, x_send, x_recv).wait_recv()

    pack_chunk(1)
    pl.semaphore_wait(barrier, 2 * n_remote + 7 + 4)
    x_start(1)
    pack_chunk(0)

    cols[...] = jnp.zeros_like(cols)
    for a in range(LATS):
        cols[4 * a : 4 * a + 4, 0:LONS] = flux_ref[a]
    cols[64 : 64 + LATS, 0:LONS] = land_ref[...].astype(F32)
    colt[...] = jnp.transpose(cols[...], (1, 0))
    drv[3:15, 176:192, :] = jnp.zeros((LATS, 16, 256), BF16)
    drv[3:15, :, 128:256] = jnp.zeros((LATS, ROWS, 128), BF16)
    for a in range(LATS):
        total = oc_ref[a].astype(F32)
        for f in range(4):
            total = total + colt[0:LONS, 4 * a + f : 4 * a + f + 1] * embed_ref[f : f + 1, :]
        drv[a + 3, 0:LONS, 0:OC] = total.astype(BF16)

    lat_low = pltpu.make_async_remote_copy(
        src_ref=drv.at[pl.ds(12, 3)], dst_ref=drv.at[pl.ds(0, 3)], send_sem=h_send.at[0],
        recv_sem=h_recv.at[0], device_id=lat_dev(1), device_id_type=MESH,
    )
    lat_high = pltpu.make_async_remote_copy(
        src_ref=drv.at[pl.ds(3, 3)], dst_ref=drv.at[pl.ds(15, 3)], send_sem=h_send.at[1],
        recv_sem=h_recv.at[1], device_id=lat_dev(-1), device_id_type=MESH,
    )
    lat_low.start()
    lat_high.start()

    sgs[...] = jnp.zeros_like(sgs)
    sgs[0:CB] = sgain_ref[...]
    sgs[CB : 2 * CB] = sgain_ref[...]
    sg2[...] = jnp.transpose(sgs[...], (1, 0))
    fws[...] = jnp.zeros_like(fws)
    fws[0:4] = fw_ref[...].astype(F32)
    fwt = fws[...].astype(BF16)
    cker[...] = jnp.zeros_like(cker)
    for i in range(7):
        cker[8 * i : 8 * i + 7, 0:OC] = ck_ref[i]

    leg_copy.wait()
    new = lax.broadcasted_iota(jnp.int32, (C, C), 0)
    old = lax.broadcasted_iota(jnp.int32, (C, C), 1)
    order = (old == lax.rem(new, 32) * LATS + new // 32).astype(F32).astype(BF16)

    def permute(m, carry):
        table = leg[m]
        leg_p[m] = lax.dot_general(
            table, order, (((1,), (1,)), ((), ())), preferred_element_type=F32
        ).astype(BF16)
        leg_t[m] = lax.dot_general(
            order, table, (((1,), (1,)), ((), ())), preferred_element_type=F32
        ).astype(BF16)
        return carry

    lax.fori_loop(0, LATS, permute, 0)

    slot = 2 * yz + h

    def z_copy(k, j):
        return pltpu.make_async_remote_copy(
            src_ref=spec[k].at[j], dst_ref=rspec[k].at[slot], send_sem=z_send.at[k],
            recv_sem=z_recv.at[k], device_id=mode_dev(j), device_id_type=MESH,
        )

    def z_local(k):
        return pltpu.make_async_copy(spec[k].at[a_id], rspec[k].at[slot], loc_sem.at[2 + k])

    lane24 = lax.broadcasted_iota(jnp.int32, (MODES, 128), 1)
    blank = jnp.zeros((8, 128), F32)

    def share(low, high):
        return jnp.where(lane24 < 64, low, pltpu.roll(high, 64, axis=1))

    def forward(k):
        width = CHUNKS[k][2]

        def step(i, carry):
            yb = lax.rem(y0 + i, 4)
            lhs = tf[pl.ds(pl.multiple_of(yb * 192, 16), 192), :]
            halves = [
                jnp.dot(lhs, got[k][s].reshape(4 * ROWS, width), preferred_element_type=F32)
                for s in range(2)
            ]
            for n in range(8):
                part = slice(MODES * n, MODES * n + MODES)
                low, high = halves[0][part], halves[1][part]
                if k == 0:
                    both = jnp.concatenate([low, high], axis=0)
                else:
                    tile = share(low[:, 128:256], high[:, 128:256])
                    both = jnp.concatenate([low[:, 0:128], high[:, 0:128], tile, blank], axis=0)
                spec[k][yb * 8 + n] = both.astype(BF16)

            def send(n, c2):
                j = yb * 8 + lax.rem(2 * z0 + n, 8)
                mine = self_peer & (j == a_id)

                @pl.when(jnp.logical_not(mine))
                def _():
                    z_copy(k, j).start()

                @pl.when(mine)
                def _():
                    z_local(k).start()

                return c2

            lax.fori_loop(0, 8, send, 0)
            return carry

        lax.fori_loop(0, 4, step, 0)

    def peers_all(k, send, recv, act):
        @pl.when(self_peer)
        def _():
            act(covers(rspec[k].at[pl.ds(0, PEERS - 1)], send.at[k], recv.at[k]))

        @pl.when(jnp.logical_not(self_peer))
        def _():
            act(covers(rspec[k], send.at[k], recv.at[k]))

    tf_copy.wait()
    x_wait(1)
    x_start(0)
    forward(1)

    lat_low.wait_recv()
    lat_high.wait_recv()

    @pl.when(a_id == 0)
    def _():
        drv[0:3] = jnp.zeros((3, ROWS, 256), BF16)

    @pl.when(a_id == 31)
    def _():
        drv[15:18] = jnp.zeros((3, ROWS, 256), BF16)

    edge_l[...] = drv[:, 0:16, :]
    edge_r[...] = drv[:, 176:192, :]
    lon_low = pltpu.make_async_remote_copy(
        src_ref=edge_r, dst_ref=halo_l, send_sem=h_send.at[2],
        recv_sem=h_recv.at[2], device_id=lon_dev(1), device_id_type=MESH,
    )
    lon_high = pltpu.make_async_remote_copy(
        src_ref=edge_l, dst_ref=halo_r, send_sem=h_send.at[3],
        recv_sem=h_recv.at[3], device_id=lon_dev(-1), device_id_type=MESH,
    )
    lon_low.start()
    lon_high.start()

    x_wait(0)
    forward(0)

    lon_low.wait_recv()
    lon_high.wait_recv()

    def place(r, carry):
        cpad[r, 0:8, :] = pltpu.roll(halo_l[r].astype(F32), 15, axis=0)[0:8]
        cpad[r, 176:192, :] = jnp.zeros((16, 256), F32)
        cpad[r, 183:189, :] = halo_r[r].astype(F32)[0:6]
        cpad[r, 3:183, :] = drv[r, 0:LONS, :].astype(F32)
        return carry

    lax.fori_loop(0, LATS + 6, place, 0)
    lane = lax.broadcasted_iota(jnp.int32, (ROWS, 256), 1)

    def ocean(a, carry):
        halves = []
        for t in range(2):
            part = slice(128 * t, 128 * t + 128)
            total = None
            for j in range(7):
                acc = None
                for i in range(7):
                    term = cker[8 * i + j : 8 * i + j + 1, part] * cpad[a + i, :, part]
                    acc = term if acc is None else acc + term
                if j:
                    acc = pltpu.roll(acc, ROWS - j, axis=0)
                total = acc if total is None else total + acc
            halves.append(total)
        conv = jnp.concatenate(halves, axis=1)
        mean = jnp.sum(conv, axis=1, keepdims=True) * (1.0 / OC)
        centred = jnp.where(lane < OC, conv - mean, 0.0)
        var = jnp.sum(centred * centred, axis=1, keepdims=True) * (1.0 / OC)
        scaled = centred * lax.rsqrt(var + 1e-05)
        normed = (scaled[:, 0:OC] * ngain_ref[...]).astype(BF16)
        hidden = jax.nn.gelu(
            jnp.dot(normed, up_ref[...], preferred_element_type=F32)
        ).astype(BF16)
        update = lax.dot_general(
            hidden, down_ref[...], (((1,), (1,)), ((), ())), preferred_element_type=F32
        )
        mask_lane = lax.broadcasted_iota(jnp.int32, (ROWS, 128), 1)
        sea = jnp.sum(
            jnp.where(mask_lane == 64 + a, colt[0:ROWS, :], 0.0), axis=1, keepdims=True
        )
        held = drv[a + 3, :, 0:OC].astype(F32) + update
        oc_out[a] = jnp.where(sea == 1.0, held, 0.0)[0:LONS].astype(BF16)
        return carry

    lax.fori_loop(0, LATS, ocean, 0)

    def add_halves(k):

        def step(i, carry):
            both = rspec[k][2 * i].astype(F32) + rspec[k][2 * i + 1].astype(F32)
            at = pl.ds(pl.multiple_of(i * 48, 8), 48)
            if k == 0:
                for t in range(3):
                    rsum[t, at, :] = both[:, 128 * t : 128 * t + 128]
            else:
                rsum[3, at, :] = both[0:48]
                tile = both[48:72]
                rsum[4, at, :] = jnp.concatenate([tile, pltpu.roll(tile, 64, axis=1)], axis=0)
            return carry

        lax.fori_loop(0, 16, step, 0)

    def z_wait(k):
        peers_all(k, z_send, z_recv, lambda copy: copy.wait_recv())

        @pl.when(self_peer)
        def _():
            z_local(k).wait()

    spans = ((range(0, 8), 0, 3), (range(8, LATS), 3, 5))

    def gather(k, m):
        bands, first, end = spans[k]
        rows = {
            (p, t): rsum[t, pl.ds(2 * m + p, 32, stride=MODES), :]
            for p in range(2)
            for t in range(first, end)
        }
        blocks = []
        for a in bands:
            moves = [(p, CB * a, CB * p, CB) for p in range(2)]
            blocks.append(move_lanes(moves, 1, lambda key, t: rows[key, t], 32)[0])
        return jnp.concatenate(blocks, axis=0).astype(BF16)

    def scatter(k, m, synth):
        bands, first, end = spans[k]
        for p in range(2):
            moves = [(n, CB * p, CB * a - 128 * first, CB) for n, a in enumerate(bands)]
            tiles = move_lanes(
                moves, end - first, lambda key, t: synth[32 * key : 32 * key + 32], 32
            )
            for t, value in enumerate(tiles):
                ssum[first + t, pl.ds(2 * m + p, 32, stride=MODES), :] = value

    def each_mode(work):
        def go(i, carry):
            for n in range(3):
                work(3 * i + n)
            return carry

        lax.fori_loop(0, LATS // 3, go, 0)

    def early(m):
        coef[m] = jnp.dot(leg_p[m, :, 256:384], gather(1, m), preferred_element_type=F32)

    def middle(m):
        coeffs = coef[m] + jnp.dot(leg_p[m, :, 0:256], gather(0, m), preferred_element_type=F32)
        filtered = (coeffs * sg2[...]).astype(BF16)
        filt[m] = filtered
        scatter(0, m, jnp.dot(leg_t[m, 0:256, :], filtered, preferred_element_type=F32))

    def late(m):
        scatter(1, m, jnp.dot(leg_t[m, 256:384, :], filt[m], preferred_element_type=F32))

    z_wait(1)
    add_halves(1)
    each_mode(early)
    z_wait(0)
    add_halves(0)
    each_mode(middle)

    def zi_copy(k, j):
        return pltpu.make_async_remote_copy(
            src_ref=syn[k].at[j // 2], dst_ref=rsyn[k].at[a_id], send_sem=zi_send.at[k],
            recv_sem=zi_recv.at[k], device_id=band_dev(j), device_id_type=MESH,
        )

    def zi_local(k):
        return pltpu.make_async_copy(syn[k].at[yz], rsyn[k].at[a_id], loc_sem.at[4 + k])

    def back(k):

        def step(i, carry):
            b = lax.rem(y0 + i // 4, 4) * 4 + lax.rem(z0 + i, 4)
            at = pl.ds(pl.multiple_of(b * 48, 8), 48)
            if k == 0:
                for t in range(3):
                    syn[k][b, :, 128 * t : 128 * t + 128] = ssum[t, at, :].astype(BF16)
            else:
                last = ssum[4, at, :]
                tile = share(last[0:MODES], last[MODES:48])
                both = jnp.concatenate([ssum[3, at, :], tile, blank], axis=0)
                syn[k][b] = both.astype(BF16)
            for n in range(2):
                j = 2 * b + n
                mine = self_peer & (j == 2 * yz + h)

                @pl.when(jnp.logical_not(mine))
                def _():
                    zi_copy(k, j).start()

                @pl.when(mine)
                def _():
                    zi_local(k).start()

            return carry

        lax.fori_loop(0, 16, step, 0)

    back(0)
    each_mode(late)
    back(1)

    def zi_wait(k):
        peers_all(k, zi_send, zi_recv, lambda copy: copy.wait_recv())

        @pl.when(self_peer)
        def _():
            zi_local(k).wait()

    def xi_copy(k, q):
        return pltpu.make_async_remote_copy(
            src_ref=gs[k].at[q], dst_ref=rg[k].at[me], send_sem=xi_send.at[k],
            recv_sem=xi_recv.at[k], device_id=row_dev(q), device_id_type=MESH,
        )

    def xi_local(k):
        return pltpu.make_async_copy(gs[k].at[me], rg[k].at[me], loc_sem.at[6 + k])

    def inverse(k):
        def regroup(i, carry):
            first = rsyn[k][2 * i].astype(F32)
            second = rsyn[k][2 * i + 1].astype(F32)
            for s in range(2):
                part = slice(MODES * s, MODES * s + MODES)
                at = pl.ds(pl.multiple_of(i * 48, 16), 48)
                both = jnp.concatenate([first[part], second[part]], axis=0)
                if k == 0:
                    sy[k][s, at, :] = both.astype(BF16)
                else:
                    sy[k][s, at, 0:128] = both.astype(BF16)
                    both = jnp.concatenate([first[48:72], second[48:72]], axis=0)
                    if s:
                        both = pltpu.roll(both, 64, axis=1)
                    sy[k][s, at, 128:256] = both.astype(BF16)
            return carry

        lax.fori_loop(0, 16, regroup, 0)

        def step(i, carry):
            xb = lax.rem(x + i, 4)
            lhs = ti[pl.ds(pl.multiple_of(xb * ROWS, 16), ROWS), :]
            for s in range(2):
                q = 2 * xb + s
                gs[k][q] = jnp.dot(lhs, sy[k][s], preferred_element_type=F32).astype(BF16)

                @pl.when(q != me)
                def _():
                    xi_copy(k, q).start()

                @pl.when(q == me)
                def _():
                    xi_local(k).start()

            return carry

        lax.fori_loop(0, 4, step, 0)

    def xi_wait(k):
        x_all(k, xi_send, xi_recv).wait_recv()
        xi_local(k).wait()

    def finish(k):
        a0, na, width = CHUNKS[k]
        for a in range(na):
            moves = [(q, CB * a, CB * q, CB) for q in range(8)]
            tiles = move_lanes(
                moves, 3,
                lambda key, t: rg[k][key, :, 128 * t : 128 * t + 128].astype(F32), ROWS,
            )
            grid = jnp.concatenate(tiles, axis=1)
            mixed = forced[a0 + a].astype(F32) + grid
            active = jax.nn.gelu(mixed).astype(BF16)
            result = mixed + jnp.dot(active, mix_ref[...], preferred_element_type=F32)
            result = result.astype(BF16)
            atm_out[a0 + a] = result[0:LONS]
            fluxes = lax.dot_general(
                fwt, result, (((1,), (1,)), ((), ())), preferred_element_type=F32
            )
            flux_out[a0 + a] = fluxes[0:4, 0:LONS]

    ti_copy.wait()
    zi_wait(0)
    inverse(0)
    xi_wait(0)
    finish(0)
    zi_wait(1)
    inverse(1)
    xi_wait(1)
    finish(1)

    for k in range(2):
        x_all(k, x_send, x_recv).wait_send()
        x_all(k, xi_send, xi_recv).wait_send()
        peers_all(k, z_send, z_recv, lambda copy: copy.wait_send())
        peers_all(k, zi_send, zi_recv, lambda copy: copy.wait_send())
    for copy in (lat_low, lat_high, lon_low, lon_high):
        copy.wait_send()


def local(
    atmosphere, ocean_state, surface_flux, land_sea, surface_read, surface_gain, legendre,
    spectral_gain, mixing, flux_weight, flux_embed, conv_kernel, norm_gain, ocean_up, ocean_down,
):
    forward_table, inverse_table = lon_tables()
    vm = pl.BlockSpec(memory_space=pltpu.VMEM)
    hbm = pl.BlockSpec(memory_space=pl.ANY)
    wide = [w for _, _, w in CHUNKS]

    def pair(*dims):
        return [pltpu.VMEM(dims + (w,), BF16) for w in wide]

    def message(count):
        return [pltpu.VMEM((count, 48, 384), BF16), pltpu.VMEM((count, 80, 128), BF16)]

    dma = pltpu.SemaphoreType.DMA
    atm_next, flux_next, ocean_next = pl.pallas_call(
        body,
        out_shape=(
            jax.ShapeDtypeStruct((LATS, LONS, C), BF16),
            jax.ShapeDtypeStruct((LATS, 4, LONS), F32),
            jax.ShapeDtypeStruct((LATS, LONS, OC), BF16),
        ),
        in_specs=[vm] * 6 + [hbm] + [vm] * 8 + [hbm] * 2,
        out_specs=(vm, vm, vm),
        scratch_shapes=[
            pltpu.VMEM((2 * M, 4 * ROWS), BF16),
            pltpu.VMEM((4 * ROWS, 2 * M), BF16),
            pltpu.VMEM((LATS, C, C), BF16),
            pltpu.VMEM((LATS, C, C), BF16),
            pltpu.VMEM((LATS, C, C), BF16),
            pltpu.VMEM((LATS, ROWS, C), BF16),
            *pair(8, ROWS),
            *pair(2, 4, ROWS),
            *message(PEERS),
            *message(PEERS),
            pltpu.VMEM((5, 768, 128), F32),
            pltpu.VMEM((5, 768, 128), F32),
            *message(16),
            *message(PEERS),
            *pair(2, 768),
            *pair(8, ROWS),
            *pair(8, ROWS),
            pltpu.VMEM((LATS, C, 128), F32),
            pltpu.VMEM((LATS, C, 128), BF16),
            pltpu.VMEM((128, C), F32),
            pltpu.VMEM((C, 128), F32),
            pltpu.VMEM((128, 256), F32),
            pltpu.VMEM((256, 128), F32),
            pltpu.VMEM((16, C), F32),
            pltpu.VMEM((LATS + 6, ROWS, 256), BF16),
            pltpu.VMEM((LATS + 6, 16, 256), BF16),
            pltpu.VMEM((LATS + 6, 16, 256), BF16),
            pltpu.VMEM((LATS + 6, 16, 256), BF16),
            pltpu.VMEM((LATS + 6, 16, 256), BF16),
            pltpu.VMEM((LATS + 6, ROWS, 256), F32),
            pltpu.VMEM((56, 256), F32),
            dma((3,)), dma((2,)), dma((2,)), dma((2,)), dma((2,)), dma((2,)), dma((2,)),
            dma((2,)), dma((2,)), dma((4,)), dma((4,)), dma((8,)),
        ],
        compiler_params=pltpu.CompilerParams(
            collective_id=0, has_side_effects=True, vmem_limit_bytes=VMEM_LIMIT
        ),
        name="window",
    )(
        atmosphere, ocean_state,
        jnp.transpose(surface_flux, (1, 0, 2)), land_sea, surface_read,
        surface_gain.reshape(3, 128), legendre, spectral_gain.T, mixing, flux_weight.T, flux_embed,
        conv_kernel, norm_gain.reshape(1, OC), ocean_up, ocean_down.T,
        jnp.asarray(forward_table), jnp.asarray(inverse_table),
    )
    return atm_next, jnp.transpose(flux_next, (1, 0, 2)), ocean_next


def solution(mesh):
    grid = P("atm", ("ocn", "ch"), None)
    return jax.shard_map(
        local,
        mesh=mesh,
        in_specs=(
            grid, grid, P(None, "atm", ("ocn", "ch")), P("atm", ("ocn", "ch")), P(), P(),
            P("atm", None, None), P(None, ("ocn", "ch")), P(), P(), P(), P(), P(), P(), P(),
        ),
        out_specs=(grid, P(None, "atm", ("ocn", "ch")), grid),
        check_vma=False,
    )
```

```python
import math

import jax
import jax.numpy as jnp
import ml_dtypes
import numpy as np
from jax import lax
from jax.experimental import pallas as pl
from jax.experimental.pallas import tpu as pltpu
from jax.sharding import PartitionSpec as P

M = 384
NLON = 1440
C = 384
OC = 200
HID = 800
LATS = 12
LONS = 180
ROWS = 192
CB = 48
PEERS = 32
MODES = 24
CHUNKS = ((0, 8, 384), (8, 4, 256))
MESH = pl.DeviceIdType.MESH
F32 = jnp.float32
BF16 = jnp.bfloat16
VMEM_LIMIT = 60 * 2**20


def lon_tables():
    lon = np.arange(NLON, dtype=np.int64)
    wave = np.arange(M, dtype=np.int64)
    phase = (lon[:, None] * wave[None, :]) % NLON
    angle = phase.astype(np.float32) * np.float32(2.0 * math.pi / NLON)
    table = np.stack([np.cos(angle), -np.sin(angle)], axis=2) * np.float32(NLON**-0.5)
    table = table.astype(np.float32).reshape(4, 2, LONS, 2 * M).transpose(1, 0, 2, 3)
    padded = np.zeros((2, 4, ROWS, 2 * M), np.float32)
    padded[:, :, :LONS] = table
    inverse = padded.reshape(2, 4 * ROWS, 2 * M).astype(ml_dtypes.bfloat16)
    return np.ascontiguousarray(inverse.transpose(0, 2, 1)), inverse


def segments(src, dst, count):
    out = []
    done = 0
    while done < count:
        s, d = src + done, dst + done
        step = min(count - done, 128 - s % 128, 128 - d % 128)
        out.append((s // 128, d // 128, (d - s) % 128, d % 128, d % 128 + step))
        done += step
    return out


def move_lanes(moves, tiles, get, rows):
    lane = lax.broadcasted_iota(jnp.int32, (rows, 128), 1)
    out = [None] * tiles
    for key, src, dst, count in moves:
        for s_tile, d_tile, shift, low, high in segments(src, dst, count):
            piece = get(key, s_tile)
            if shift:
                piece = pltpu.roll(piece, shift, axis=1)
            if out[d_tile] is None:
                if low == 0:
                    out[d_tile] = jnp.where(lane < high, piece, 0.0)
                else:
                    out[d_tile] = jnp.where((lane >= low) & (lane < high), piece, 0.0)
            else:
                out[d_tile] = jnp.where((lane >= low) & (lane < high), piece, out[d_tile])
    return out


def body(
    atm_ref, oc_ref, flux_ref, land_ref, read_ref, gain_ref, leg_hbm, sgain_ref, mix_ref, fw_ref,
    embed_ref, ck_ref, ngain_ref, up_ref, down_ref, tf_hbm, ti_hbm,
    atm_out, flux_out, oc_out,
    tf, ti, leg, leg_p, leg_t, forced,
    pack_a, pack_b, got_a, got_b, spec_a, spec_b, rspec_a, rspec_b, rsum, ssum,
    syn_a, syn_b, rsyn_a, rsyn_b, sy_a, sy_b, gs_a, gs_b, rg_a, rg_b,
    coef, filt, sgs, sg2, cols, colt, fws, drv, edge_l, edge_r, halo_l, halo_r, cpad, cker,
    in_sem, x_send, x_recv, z_send, z_recv, zi_send, zi_recv, xi_send, xi_recv, h_send, h_recv, loc_sem,
):
    pack, got, spec, rspec = (pack_a, pack_b), (got_a, got_b), (spec_a, spec_b), (rspec_a, rspec_b)
    syn, rsyn, sy, gs, rg = (syn_a, syn_b), (rsyn_a, rsyn_b), (sy_a, sy_b), (gs_a, gs_b), (rg_a, rg_b)
    a_id = lax.axis_index("atm")
    x = lax.axis_index("ocn")
    h = lax.axis_index("ch")
    core = lax.rem(a_id, 2)
    yz = a_id // 2
    y0 = yz // 4
    z0 = lax.rem(yz, 4)
    me = 2 * x + core
    lon_block = 2 * x + h
    self_peer = core == h
    n_remote = PEERS - self_peer.astype(jnp.int32)

    tf_copy = pltpu.make_async_copy(tf_hbm.at[h], tf, in_sem.at[0])
    ti_copy = pltpu.make_async_copy(ti_hbm.at[h], ti, in_sem.at[1])
    leg_copy = pltpu.make_async_copy(leg_hbm, leg, in_sem.at[2])
    tf_copy.start()
    leg_copy.start()
    ti_copy.start()

    def row_dev(q):
        return {"atm": 2 * yz + lax.rem(q, 2), "ocn": q // 2, "ch": h}

    def mode_dev(j):
        return {"atm": j, "ocn": x, "ch": core}

    def band_dev(j):
        return {"atm": (j // 2) * 2 + h, "ocn": x, "ch": lax.rem(j, 2)}

    def lat_dev(step):
        return {"atm": lax.rem(a_id + step + 32, 32), "ocn": x, "ch": h}

    def lon_dev(step):
        b = lax.rem(lon_block + step + 8, 8)
        return {"atm": a_id, "ocn": b // 2, "ch": lax.rem(b, 2)}

    barrier = pltpu.get_barrier_semaphore()

    def greet(device):
        pl.semaphore_signal(barrier, inc=1, device_id=device, device_id_type=MESH)

    def greet_row(i, carry):
        greet(row_dev(lax.rem(me + i, 8)))
        return carry

    lax.fori_loop(1, 8, greet_row, 0)
    for step in (-1, 1):
        greet(lat_dev(step))
        greet(lon_dev(step))

    def greet_peers(j, carry):
        @pl.when(jnp.logical_not(self_peer & (j == a_id)))
        def _():
            greet(mode_dev(j))

        @pl.when(jnp.logical_not(self_peer & (j == 2 * yz + h)))
        def _():
            greet(band_dev(j))

        return carry

    lax.fori_loop(0, PEERS, greet_peers, 0)

    forced[:, 176:192, :] = jnp.zeros((LATS, 16, C), BF16)

    read_row = read_ref[...].astype(F32).reshape(1, OC)

    def force(a, carry):
        seen = oc_ref[a].astype(F32) * read_row
        surface = jnp.sum(seen, axis=1, keepdims=True)
        for t in range(3):
            part = slice(128 * t, 128 * t + 128)
            total = atm_ref[a, :, part].astype(F32) + surface * gain_ref[t : t + 1, :]
            forced[a, 0:LONS, part] = total.astype(BF16)
        return carry

    lax.fori_loop(0, LATS, force, 0)

    def pack_chunk(k):
        a0, na, width = CHUNKS[k]

        def rows_step(rb, carry):
            r0 = pl.multiple_of(rb * 48, 16)
            held = {}
            for a in range(na):
                for t in range(3):
                    held[a, t] = forced[a0 + a, pl.ds(r0, 48), 128 * t : 128 * t + 128].astype(F32)
            for q in range(8):
                moves = [(a, CB * q, CB * a, CB) for a in range(na)]
                tiles = move_lanes(moves, width // 128, lambda key, t: held[key, t], 48)
                for t, value in enumerate(tiles):
                    pack[k][q, pl.ds(r0, 48), 128 * t : 128 * t + 128] = value.astype(BF16)
            return carry

        lax.fori_loop(0, 4, rows_step, 0)

    def x_copy(k, q):
        return pltpu.make_async_remote_copy(
            src_ref=pack[k].at[q], dst_ref=got[k].at[core, x], send_sem=x_send.at[k],
            recv_sem=x_recv.at[k], device_id=row_dev(q), device_id_type=MESH,
        )

    def x_start(k):
        pltpu.make_async_copy(pack[k].at[me], got[k].at[core, x], loc_sem.at[k]).start()

        def go(i, carry):
            x_copy(k, lax.rem(me + i, 8)).start()
            return carry

        lax.fori_loop(1, 8, go, 0)

    def covers(ref, send, recv):
        return pltpu.make_async_remote_copy(
            src_ref=ref, dst_ref=ref, send_sem=send, recv_sem=recv,
            device_id=lat_dev(1), device_id_type=MESH,
        )

    def x_all(k, send, recv):
        return covers(pack[k].at[pl.ds(0, 7)], send.at[k], recv.at[k])

    def x_wait(k):
        pltpu.make_async_copy(pack[k].at[me], got[k].at[core, x], loc_sem.at[k]).wait()
        x_all(k, x_send, x_recv).wait_recv()

    pack_chunk(1)
    pl.semaphore_wait(barrier, 2 * n_remote + 7 + 4)
    x_start(1)
    pack_chunk(0)

    cols[...] = jnp.zeros_like(cols)
    for a in range(LATS):
        cols[4 * a : 4 * a + 4, 0:LONS] = flux_ref[a]
    cols[64 : 64 + LATS, 0:LONS] = land_ref[...].astype(F32)
    colt[...] = jnp.transpose(cols[...], (1, 0))
    drv[3:15, 176:192, :] = jnp.zeros((LATS, 16, 256), BF16)
    drv[3:15, :, 128:256] = jnp.zeros((LATS, ROWS, 128), BF16)
    for a in range(LATS):
        total = oc_ref[a].astype(F32)
        for f in range(4):
            total = total + colt[0:LONS, 4 * a + f : 4 * a + f + 1] * embed_ref[f : f + 1, :]
        drv[a + 3, 0:LONS, 0:OC] = total.astype(BF16)

    lat_low = pltpu.make_async_remote_copy(
        src_ref=drv.at[pl.ds(12, 3)], dst_ref=drv.at[pl.ds(0, 3)], send_sem=h_send.at[0],
        recv_sem=h_recv.at[0], device_id=lat_dev(1), device_id_type=MESH,
    )
    lat_high = pltpu.make_async_remote_copy(
        src_ref=drv.at[pl.ds(3, 3)], dst_ref=drv.at[pl.ds(15, 3)], send_sem=h_send.at[1],
        recv_sem=h_recv.at[1], device_id=lat_dev(-1), device_id_type=MESH,
    )
    lat_low.start()
    lat_high.start()

    sgs[...] = jnp.zeros_like(sgs)
    sgs[0:CB] = sgain_ref[...]
    sgs[CB : 2 * CB] = sgain_ref[...]
    sg2[...] = jnp.transpose(sgs[...], (1, 0))
    fws[...] = jnp.zeros_like(fws)
    fws[0:4] = fw_ref[...].astype(F32)
    fwt = fws[...].astype(BF16)
    cker[...] = jnp.zeros_like(cker)
    for i in range(7):
        cker[8 * i : 8 * i + 7, 0:OC] = ck_ref[i]

    leg_copy.wait()
    new = lax.broadcasted_iota(jnp.int32, (C, C), 0)
    old = lax.broadcasted_iota(jnp.int32, (C, C), 1)
    order = (old == lax.rem(new, 32) * LATS + new // 32).astype(F32).astype(BF16)

    def permute(m, carry):
        table = leg[m]
        leg_p[m] = lax.dot_general(
            table, order, (((1,), (1,)), ((), ())), preferred_element_type=F32
        ).astype(BF16)
        leg_t[m] = lax.dot_general(
            order, table, (((1,), (1,)), ((), ())), preferred_element_type=F32
        ).astype(BF16)
        return carry

    lax.fori_loop(0, LATS, permute, 0)

    slot = 2 * yz + h

    def z_copy(k, j):
        return pltpu.make_async_remote_copy(
            src_ref=spec[k].at[j], dst_ref=rspec[k].at[slot], send_sem=z_send.at[k],
            recv_sem=z_recv.at[k], device_id=mode_dev(j), device_id_type=MESH,
        )

    def z_local(k):
        return pltpu.make_async_copy(spec[k].at[a_id], rspec[k].at[slot], loc_sem.at[2 + k])

    lane24 = lax.broadcasted_iota(jnp.int32, (MODES, 128), 1)
    blank = jnp.zeros((8, 128), F32)

    def share(low, high):
        return jnp.where(lane24 < 64, low, pltpu.roll(high, 64, axis=1))

    def forward(k):
        width = CHUNKS[k][2]

        def step(i, carry):
            yb = lax.rem(y0 + i, 4)
            lhs = tf[pl.ds(pl.multiple_of(yb * 192, 16), 192), :]
            halves = [
                jnp.dot(lhs, got[k][s].reshape(4 * ROWS, width), preferred_element_type=F32)
                for s in range(2)
            ]
            for n in range(8):
                part = slice(MODES * n, MODES * n + MODES)
                low, high = halves[0][part], halves[1][part]
                if k == 0:
                    both = jnp.concatenate([low, high], axis=0)
                else:
                    tile = share(low[:, 128:256], high[:, 128:256])
                    both = jnp.concatenate([low[:, 0:128], high[:, 0:128], tile, blank], axis=0)
                spec[k][yb * 8 + n] = both.astype(BF16)

            def send(n, c2):
                j = yb * 8 + lax.rem(2 * z0 + n, 8)
                mine = self_peer & (j == a_id)

                @pl.when(jnp.logical_not(mine))
                def _():
                    z_copy(k, j).start()

                @pl.when(mine)
                def _():
                    z_local(k).start()

                return c2

            lax.fori_loop(0, 8, send, 0)
            return carry

        lax.fori_loop(0, 4, step, 0)

    def peers_all(k, send, recv, act):
        @pl.when(self_peer)
        def _():
            act(covers(rspec[k].at[pl.ds(0, PEERS - 1)], send.at[k], recv.at[k]))

        @pl.when(jnp.logical_not(self_peer))
        def _():
            act(covers(rspec[k], send.at[k], recv.at[k]))

    tf_copy.wait()
    x_wait(1)
    x_start(0)
    forward(1)

    lat_low.wait_recv()
    lat_high.wait_recv()

    @pl.when(a_id == 0)
    def _():
        drv[0:3] = jnp.zeros((3, ROWS, 256), BF16)

    @pl.when(a_id == 31)
    def _():
        drv[15:18] = jnp.zeros((3, ROWS, 256), BF16)

    edge_l[...] = drv[:, 0:16, :]
    edge_r[...] = drv[:, 176:192, :]
    lon_low = pltpu.make_async_remote_copy(
        src_ref=edge_r, dst_ref=halo_l, send_sem=h_send.at[2],
        recv_sem=h_recv.at[2], device_id=lon_dev(1), device_id_type=MESH,
    )
    lon_high = pltpu.make_async_remote_copy(
        src_ref=edge_l, dst_ref=halo_r, send_sem=h_send.at[3],
        recv_sem=h_recv.at[3], device_id=lon_dev(-1), device_id_type=MESH,
    )
    lon_low.start()
    lon_high.start()

    x_wait(0)
    forward(0)

    lon_low.wait_recv()
    lon_high.wait_recv()

    def place(r, carry):
        cpad[r, 0:8, :] = pltpu.roll(halo_l[r].astype(F32), 15, axis=0)[0:8]
        cpad[r, 176:192, :] = jnp.zeros((16, 256), F32)
        cpad[r, 183:189, :] = halo_r[r].astype(F32)[0:6]
        cpad[r, 3:183, :] = drv[r, 0:LONS, :].astype(F32)
        return carry

    lax.fori_loop(0, LATS + 6, place, 0)
    lane = lax.broadcasted_iota(jnp.int32, (ROWS, 256), 1)

    def ocean(a, carry):
        halves = []
        for t in range(2):
            part = slice(128 * t, 128 * t + 128)
            total = None
            for j in range(7):
                acc = None
                for i in range(7):
                    term = cker[8 * i + j : 8 * i + j + 1, part] * cpad[a + i, :, part]
                    acc = term if acc is None else acc + term
                if j:
                    acc = pltpu.roll(acc, ROWS - j, axis=0)
                total = acc if total is None else total + acc
            halves.append(total)
        conv = jnp.concatenate(halves, axis=1)
        mean = jnp.sum(conv, axis=1, keepdims=True) * (1.0 / OC)
        centred = jnp.where(lane < OC, conv - mean, 0.0)
        var = jnp.sum(centred * centred, axis=1, keepdims=True) * (1.0 / OC)
        scaled = centred * lax.rsqrt(var + 1e-05)
        normed = (scaled[:, 0:OC] * ngain_ref[...]).astype(BF16)
        hidden = jax.nn.gelu(
            jnp.dot(normed, up_ref[...], preferred_element_type=F32)
        ).astype(BF16)
        update = lax.dot_general(
            hidden, down_ref[...], (((1,), (1,)), ((), ())), preferred_element_type=F32
        )
        mask_lane = lax.broadcasted_iota(jnp.int32, (ROWS, 128), 1)
        sea = jnp.sum(
            jnp.where(mask_lane == 64 + a, colt[0:ROWS, :], 0.0), axis=1, keepdims=True
        )
        held = drv[a + 3, :, 0:OC].astype(F32) + update
        oc_out[a] = jnp.where(sea == 1.0, held, 0.0)[0:LONS].astype(BF16)
        return carry

    lax.fori_loop(0, LATS, ocean, 0)

    def add_halves(k):

        def step(i, carry):
            both = rspec[k][2 * i].astype(F32) + rspec[k][2 * i + 1].astype(F32)
            at = pl.ds(pl.multiple_of(i * 48, 8), 48)
            if k == 0:
                for t in range(3):
                    rsum[t, at, :] = both[:, 128 * t : 128 * t + 128]
            else:
                rsum[3, at, :] = both[0:48]
                tile = both[48:72]
                rsum[4, at, :] = jnp.concatenate([tile, pltpu.roll(tile, 64, axis=1)], axis=0)
            return carry

        lax.fori_loop(0, 16, step, 0)

    def z_wait(k):
        peers_all(k, z_send, z_recv, lambda copy: copy.wait_recv())

        @pl.when(self_peer)
        def _():
            z_local(k).wait()

    spans = ((range(0, 8), 0, 3), (range(8, LATS), 3, 5))

    def gather(k, m):
        bands, first, end = spans[k]
        rows = {
            (p, t): rsum[t, pl.ds(2 * m + p, 32, stride=MODES), :]
            for p in range(2)
            for t in range(first, end)
        }
        blocks = []
        for a in bands:
            moves = [(p, CB * a, CB * p, CB) for p in range(2)]
            blocks.append(move_lanes(moves, 1, lambda key, t: rows[key, t], 32)[0])
        return jnp.concatenate(blocks, axis=0).astype(BF16)

    def scatter(k, m, synth):
        bands, first, end = spans[k]
        for p in range(2):
            moves = [(n, CB * p, CB * a - 128 * first, CB) for n, a in enumerate(bands)]
            tiles = move_lanes(
                moves, end - first, lambda key, t: synth[32 * key : 32 * key + 32], 32
            )
            for t, value in enumerate(tiles):
                ssum[first + t, pl.ds(2 * m + p, 32, stride=MODES), :] = value

    def each_mode(work):
        def go(i, carry):
            for n in range(3):
                work(3 * i + n)
            return carry

        lax.fori_loop(0, LATS // 3, go, 0)

    def early(m):
        coef[m] = jnp.dot(leg_p[m, :, 256:384], gather(1, m), preferred_element_type=F32)

    def middle(m):
        coeffs = coef[m] + jnp.dot(leg_p[m, :, 0:256], gather(0, m), preferred_element_type=F32)
        filtered = (coeffs * sg2[...]).astype(BF16)
        filt[m] = filtered
        scatter(0, m, jnp.dot(leg_t[m, 0:256, :], filtered, preferred_element_type=F32))

    def late(m):
        scatter(1, m, jnp.dot(leg_t[m, 256:384, :], filt[m], preferred_element_type=F32))

    z_wait(1)
    add_halves(1)
    each_mode(early)
    z_wait(0)
    add_halves(0)
    each_mode(middle)

    def zi_copy(k, j):
        return pltpu.make_async_remote_copy(
            src_ref=syn[k].at[j // 2], dst_ref=rsyn[k].at[a_id], send_sem=zi_send.at[k],
            recv_sem=zi_recv.at[k], device_id=band_dev(j), device_id_type=MESH,
        )

    def zi_local(k):
        return pltpu.make_async_copy(syn[k].at[yz], rsyn[k].at[a_id], loc_sem.at[4 + k])

    def back(k, fill, send):
        def step(i, carry):
            b = lax.rem(y0 + i // 4, 4) * 4 + lax.rem(z0 + i, 4)
            at = pl.ds(pl.multiple_of(b * 48, 8), 48)
            if fill and k == 0:
                for t in range(3):
                    syn[k][b, :, 128 * t : 128 * t + 128] = ssum[t, at, :].astype(BF16)
            elif fill:
                last = ssum[4, at, :]
                tile = share(last[0:MODES], last[MODES:48])
                both = jnp.concatenate([ssum[3, at, :], tile, blank], axis=0)
                syn[k][b] = both.astype(BF16)
            for n in range(2 if send else 0):
                j = 2 * b + n
                mine = self_peer & (j == 2 * yz + h)

                @pl.when(jnp.logical_not(mine))
                def _():
                    zi_copy(k, j).start()

                @pl.when(mine)
                def _():
                    zi_local(k).start()

            return carry

        lax.fori_loop(0, 16, step, 0)

    back(0, True, True)
    each_mode(late)
    back(1, True, False)
    peers_all(0, zi_send, zi_recv, lambda copy: copy.wait_send())
    back(1, False, True)

    def zi_wait(k):
        peers_all(k, zi_send, zi_recv, lambda copy: copy.wait_recv())

        @pl.when(self_peer)
        def _():
            zi_local(k).wait()

    def xi_copy(k, q):
        return pltpu.make_async_remote_copy(
            src_ref=gs[k].at[q], dst_ref=rg[k].at[me], send_sem=xi_send.at[k],
            recv_sem=xi_recv.at[k], device_id=row_dev(q), device_id_type=MESH,
        )

    def xi_local(k):
        return pltpu.make_async_copy(gs[k].at[me], rg[k].at[me], loc_sem.at[6 + k])

    def inverse(k):
        def regroup(i, carry):
            first = rsyn[k][2 * i].astype(F32)
            second = rsyn[k][2 * i + 1].astype(F32)
            for s in range(2):
                part = slice(MODES * s, MODES * s + MODES)
                at = pl.ds(pl.multiple_of(i * 48, 16), 48)
                both = jnp.concatenate([first[part], second[part]], axis=0)
                if k == 0:
                    sy[k][s, at, :] = both.astype(BF16)
                else:
                    sy[k][s, at, 0:128] = both.astype(BF16)
                    both = jnp.concatenate([first[48:72], second[48:72]], axis=0)
                    if s:
                        both = pltpu.roll(both, 64, axis=1)
                    sy[k][s, at, 128:256] = both.astype(BF16)
            return carry

        lax.fori_loop(0, 16, regroup, 0)

        def step(i, carry):
            xb = lax.rem(x + i, 4)
            lhs = ti[pl.ds(pl.multiple_of(xb * ROWS, 16), ROWS), :]
            for s in range(2):
                q = 2 * xb + s
                gs[k][q] = jnp.dot(lhs, sy[k][s], preferred_element_type=F32).astype(BF16)

                @pl.when(q != me)
                def _():
                    xi_copy(k, q).start()

                @pl.when(q == me)
                def _():
                    xi_local(k).start()

            return carry

        lax.fori_loop(0, 4, step, 0)

    def xi_wait(k):
        x_all(k, xi_send, xi_recv).wait_recv()
        xi_local(k).wait()

    def finish(k):
        a0, na, width = CHUNKS[k]
        for a in range(na):
            moves = [(q, CB * a, CB * q, CB) for q in range(8)]
            tiles = move_lanes(
                moves, 3,
                lambda key, t: rg[k][key, :, 128 * t : 128 * t + 128].astype(F32), ROWS,
            )
            grid = jnp.concatenate(tiles, axis=1)
            mixed = forced[a0 + a].astype(F32) + grid
            active = jax.nn.gelu(mixed).astype(BF16)
            result = mixed + jnp.dot(active, mix_ref[...], preferred_element_type=F32)
            result = result.astype(BF16)
            atm_out[a0 + a] = result[0:LONS]
            fluxes = lax.dot_general(
                fwt, result, (((1,), (1,)), ((), ())), preferred_element_type=F32
            )
            flux_out[a0 + a] = fluxes[0:4, 0:LONS]

    ti_copy.wait()
    zi_wait(0)
    inverse(0)
    zi_wait(1)
    inverse(1)
    xi_wait(0)
    finish(0)
    xi_wait(1)
    finish(1)

    for k in range(2):
        x_all(k, x_send, x_recv).wait_send()
        x_all(k, xi_send, xi_recv).wait_send()
        peers_all(k, z_send, z_recv, lambda copy: copy.wait_send())
    peers_all(1, zi_send, zi_recv, lambda copy: copy.wait_send())
    for copy in (lat_low, lat_high, lon_low, lon_high):
        copy.wait_send()


def local(
    atmosphere, ocean_state, surface_flux, land_sea, surface_read, surface_gain, legendre,
    spectral_gain, mixing, flux_weight, flux_embed, conv_kernel, norm_gain, ocean_up, ocean_down,
):
    forward_table, inverse_table = lon_tables()
    vm = pl.BlockSpec(memory_space=pltpu.VMEM)
    hbm = pl.BlockSpec(memory_space=pl.ANY)
    wide = [w for _, _, w in CHUNKS]

    def pair(*dims):
        return [pltpu.VMEM(dims + (w,), BF16) for w in wide]

    def message(count):
        return [pltpu.VMEM((count, 48, 384), BF16), pltpu.VMEM((count, 80, 128), BF16)]

    dma = pltpu.SemaphoreType.DMA
    atm_next, flux_next, ocean_next = pl.pallas_call(
        body,
        out_shape=(
            jax.ShapeDtypeStruct((LATS, LONS, C), BF16),
            jax.ShapeDtypeStruct((LATS, 4, LONS), F32),
            jax.ShapeDtypeStruct((LATS, LONS, OC), BF16),
        ),
        in_specs=[vm] * 6 + [hbm] + [vm] * 8 + [hbm] * 2,
        out_specs=(vm, vm, vm),
        scratch_shapes=[
            pltpu.VMEM((2 * M, 4 * ROWS), BF16),
            pltpu.VMEM((4 * ROWS, 2 * M), BF16),
            pltpu.VMEM((LATS, C, C), BF16),
            pltpu.VMEM((LATS, C, C), BF16),
            pltpu.VMEM((LATS, C, C), BF16),
            pltpu.VMEM((LATS, ROWS, C), BF16),
            *pair(8, ROWS),
            *pair(2, 4, ROWS),
            *message(PEERS),
            *message(PEERS),
            pltpu.VMEM((5, 768, 128), F32),
            pltpu.VMEM((5, 768, 128), F32),
            *message(16),
            *message(PEERS),
            *pair(2, 768),
            *pair(8, ROWS),
            *pair(8, ROWS),
            pltpu.VMEM((LATS, C, 128), F32),
            pltpu.VMEM((LATS, C, 128), BF16),
            pltpu.VMEM((128, C), F32),
            pltpu.VMEM((C, 128), F32),
            pltpu.VMEM((128, 256), F32),
            pltpu.VMEM((256, 128), F32),
            pltpu.VMEM((16, C), F32),
            pltpu.VMEM((LATS + 6, ROWS, 256), BF16),
            pltpu.VMEM((LATS + 6, 16, 256), BF16),
            pltpu.VMEM((LATS + 6, 16, 256), BF16),
            pltpu.VMEM((LATS + 6, 16, 256), BF16),
            pltpu.VMEM((LATS + 6, 16, 256), BF16),
            pltpu.VMEM((LATS + 6, ROWS, 256), F32),
            pltpu.VMEM((56, 256), F32),
            dma((3,)), dma((2,)), dma((2,)), dma((2,)), dma((2,)), dma((2,)), dma((2,)),
            dma((2,)), dma((2,)), dma((4,)), dma((4,)), dma((8,)),
        ],
        compiler_params=pltpu.CompilerParams(
            collective_id=0, has_side_effects=True, vmem_limit_bytes=VMEM_LIMIT
        ),
        name="window",
    )(
        atmosphere, ocean_state,
        jnp.transpose(surface_flux, (1, 0, 2)), land_sea, surface_read,
        surface_gain.reshape(3, 128), legendre, spectral_gain.T, mixing, flux_weight.T, flux_embed,
        conv_kernel, norm_gain.reshape(1, OC), ocean_up, ocean_down.T,
        jnp.asarray(forward_table), jnp.asarray(inverse_table),
    )
    return atm_next, jnp.transpose(flux_next, (1, 0, 2)), ocean_next


def solution(mesh):
    grid = P("atm", ("ocn", "ch"), None)
    return jax.shard_map(
        local,
        mesh=mesh,
        in_specs=(
            grid, grid, P(None, "atm", ("ocn", "ch")), P("atm", ("ocn", "ch")), P(), P(),
            P("atm", None, None), P(None, ("ocn", "ch")), P(), P(), P(), P(), P(), P(), P(),
        ),
        out_specs=(grid, P(None, "atm", ("ocn", "ch")), grid),
        check_vma=False,
    )
```

```python
import math

import jax
import jax.numpy as jnp
import ml_dtypes
import numpy as np
from jax import lax
from jax.experimental import pallas as pl
from jax.experimental.pallas import tpu as pltpu
from jax.sharding import PartitionSpec as P

M = 384
NLON = 1440
C = 384
OC = 200
HID = 800
LATS = 12
LONS = 180
ROWS = 192
CB = 48
PEERS = 32
MODES = 24
CHUNKS = ((0, 8, 384), (8, 4, 256))
MESH = pl.DeviceIdType.MESH
F32 = jnp.float32
BF16 = jnp.bfloat16
VMEM_LIMIT = 60 * 2**20


def lon_tables():
    lon = np.arange(NLON, dtype=np.int64)
    wave = np.arange(M, dtype=np.int64)
    phase = (lon[:, None] * wave[None, :]) % NLON
    angle = phase.astype(np.float32) * np.float32(2.0 * math.pi / NLON)
    table = np.stack([np.cos(angle), -np.sin(angle)], axis=2) * np.float32(NLON**-0.5)
    table = table.astype(np.float32).reshape(4, 2, LONS, 2 * M).transpose(1, 0, 2, 3)
    padded = np.zeros((2, 4, ROWS, 2 * M), np.float32)
    padded[:, :, :LONS] = table
    inverse = padded.reshape(2, 4 * ROWS, 2 * M).astype(ml_dtypes.bfloat16)
    return np.ascontiguousarray(inverse.transpose(0, 2, 1)), inverse


def segments(src, dst, count):
    out = []
    done = 0
    while done < count:
        s, d = src + done, dst + done
        step = min(count - done, 128 - s % 128, 128 - d % 128)
        out.append((s // 128, d // 128, (d - s) % 128, d % 128, d % 128 + step))
        done += step
    return out


def move_lanes(moves, tiles, get, rows):
    lane = lax.broadcasted_iota(jnp.int32, (rows, 128), 1)
    out = [None] * tiles
    for key, src, dst, count in moves:
        for s_tile, d_tile, shift, low, high in segments(src, dst, count):
            piece = get(key, s_tile)
            if shift:
                piece = pltpu.roll(piece, shift, axis=1)
            if out[d_tile] is None:
                if low == 0:
                    out[d_tile] = jnp.where(lane < high, piece, 0.0)
                else:
                    out[d_tile] = jnp.where((lane >= low) & (lane < high), piece, 0.0)
            else:
                out[d_tile] = jnp.where((lane >= low) & (lane < high), piece, out[d_tile])
    return out


def body(
    atm_ref, oc_ref, flux_ref, land_ref, read_ref, gain_ref, leg_hbm, sgain_ref, mix_ref, fw_ref,
    embed_ref, ck_ref, ngain_ref, up_ref, down_ref, tf_hbm, ti_hbm,
    atm_out, flux_out, oc_out,
    tf, ti, leg, leg_p, leg_t, forced,
    pack_a, pack_b, got_a, got_b, gin, spec_a, spec_b, rspec_a, rspec_b, rsum, ssum,
    syn_a, syn_b, rsyn_a, rsyn_b, sy_a, sy_b, gs_a, gs_b, rg_a, rg_b,
    coef, filt, sgs, sg2, cols, colt, fws, drv, edge_l, edge_r, halo_l, halo_r, cpad, cker,
    in_sem, x_send, x_recv, z_send, z_recv, zi_send, zi_recv, xi_send, xi_recv, h_send, h_recv, loc_sem,
):
    pack, got, spec, rspec = (pack_a, pack_b), (got_a, got_b), (spec_a, spec_b), (rspec_a, rspec_b)
    syn, rsyn, sy, gs, rg = (syn_a, syn_b), (rsyn_a, rsyn_b), (sy_a, sy_b), (gs_a, gs_b), (rg_a, rg_b)
    a_id = lax.axis_index("atm")
    x = lax.axis_index("ocn")
    h = lax.axis_index("ch")
    core = lax.rem(a_id, 2)
    yz = a_id // 2
    y0 = yz // 4
    z0 = lax.rem(yz, 4)
    me = 2 * x + core
    lon_block = 2 * x + h
    self_peer = core == h
    n_remote = PEERS - self_peer.astype(jnp.int32)

    tf_copy = pltpu.make_async_copy(tf_hbm.at[h], tf, in_sem.at[0])
    ti_copy = pltpu.make_async_copy(ti_hbm.at[h], ti, in_sem.at[1])
    leg_copy = pltpu.make_async_copy(leg_hbm, leg, in_sem.at[2])
    tf_copy.start()
    leg_copy.start()
    ti_copy.start()

    def row_dev(q):
        return {"atm": 2 * yz + lax.rem(q, 2), "ocn": q // 2, "ch": h}

    def mode_dev(j):
        return {"atm": j, "ocn": x, "ch": core}

    def band_dev(j):
        return {"atm": (j // 2) * 2 + h, "ocn": x, "ch": lax.rem(j, 2)}

    def lat_dev(step):
        return {"atm": lax.rem(a_id + step + 32, 32), "ocn": x, "ch": h}

    def lon_dev(step):
        b = lax.rem(lon_block + step + 8, 8)
        return {"atm": a_id, "ocn": b // 2, "ch": lax.rem(b, 2)}

    barrier = pltpu.get_barrier_semaphore()

    def greet(device):
        pl.semaphore_signal(barrier, inc=1, device_id=device, device_id_type=MESH)

    def greet_row(i, carry):
        greet(row_dev(lax.rem(me + i, 8)))
        return carry

    lax.fori_loop(1, 8, greet_row, 0)
    for step in (-1, 1):
        greet(lat_dev(step))
        greet(lon_dev(step))

    def greet_peers(j, carry):
        @pl.when(jnp.logical_not(self_peer & (j == a_id)))
        def _():
            greet(mode_dev(j))

        @pl.when(jnp.logical_not(self_peer & (j == 2 * yz + h)))
        def _():
            greet(band_dev(j))

        return carry

    lax.fori_loop(0, PEERS, greet_peers, 0)

    forced[:, 176:192, :] = jnp.zeros((LATS, 16, C), BF16)

    read_row = read_ref[...].astype(F32).reshape(1, OC)

    def force(a, carry):
        seen = oc_ref[a].astype(F32) * read_row
        surface = jnp.sum(seen, axis=1, keepdims=True)
        for t in range(3):
            part = slice(128 * t, 128 * t + 128)
            total = atm_ref[a, :, part].astype(F32) + surface * gain_ref[t : t + 1, :]
            forced[a, 0:LONS, part] = total.astype(BF16)
        return carry

    lax.fori_loop(0, LATS, force, 0)

    def share(low, high):
        lanes = lax.broadcasted_iota(jnp.int32, low.shape, 1)
        return jnp.where(lanes < 64, low, pltpu.roll(high, 64, axis=1))

    def pack_chunk(k):
        a0, na, width = CHUNKS[k]

        def pieces(r0):
            held = {}
            for a in range(na):
                for t in range(3):
                    held[a, t] = forced[a0 + a, pl.ds(r0, 48), 128 * t : 128 * t + 128].astype(F32)
            for q in range(8):
                moves = [(a, CB * q, CB * a, CB) for a in range(na)]
                yield q, move_lanes(moves, width // 128, lambda key, t: held[key, t], 48)

        def whole_step(rb, carry):
            r0 = pl.multiple_of(rb * 48, 16)
            for q, tiles in pieces(r0):
                for t, value in enumerate(tiles):
                    pack[k][q, pl.ds(r0, 48), 128 * t : 128 * t + 128] = value.astype(BF16)
            return carry

        def shared_step(rb, carry):
            r0 = pl.multiple_of(rb * 48, 16)
            r1 = pl.multiple_of(rb * 48 + 96, 16)
            r2 = pl.multiple_of(rb * 48 + ROWS, 16)
            for (q, low), (_, high) in zip(pieces(r0), pieces(r1)):
                pack[k][q, pl.ds(r0, 48), :] = low[0].astype(BF16)
                pack[k][q, pl.ds(r1, 48), :] = high[0].astype(BF16)
                pack[k][q, pl.ds(r2, 48), :] = share(low[1], high[1]).astype(BF16)
            return carry

        if k == 0:
            lax.fori_loop(0, 4, whole_step, 0)
        else:
            lax.fori_loop(0, 2, shared_step, 0)

    def x_copy(k, q):
        return pltpu.make_async_remote_copy(
            src_ref=pack[k].at[q], dst_ref=got[k].at[core, x], send_sem=x_send.at[k],
            recv_sem=x_recv.at[k], device_id=row_dev(q), device_id_type=MESH,
        )

    def x_start(k):
        pltpu.make_async_copy(pack[k].at[me], got[k].at[core, x], loc_sem.at[k]).start()

        def go(i, carry):
            x_copy(k, lax.rem(me + i, 8)).start()
            return carry

        lax.fori_loop(1, 8, go, 0)

    def covers(ref, send, recv):
        return pltpu.make_async_remote_copy(
            src_ref=ref, dst_ref=ref, send_sem=send, recv_sem=recv,
            device_id=lat_dev(1), device_id_type=MESH,
        )

    def x_all(k, send, recv):
        return covers(pack[k].at[pl.ds(0, 7)], send.at[k], recv.at[k])

    def x_wait(k):
        pltpu.make_async_copy(pack[k].at[me], got[k].at[core, x], loc_sem.at[k]).wait()
        x_all(k, x_send, x_recv).wait_recv()

    pack_chunk(1)
    pl.semaphore_wait(barrier, 2 * n_remote + 7 + 4)
    x_start(1)
    pack_chunk(0)

    cols[...] = jnp.zeros_like(cols)
    for a in range(LATS):
        cols[4 * a : 4 * a + 4, 0:LONS] = flux_ref[a]
    cols[64 : 64 + LATS, 0:LONS] = land_ref[...].astype(F32)
    colt[...] = jnp.transpose(cols[...], (1, 0))
    drv[3:15, 176:192, :] = jnp.zeros((LATS, 16, 256), BF16)
    drv[3:15, :, 128:256] = jnp.zeros((LATS, ROWS, 128), BF16)
    for a in range(LATS):
        total = oc_ref[a].astype(F32)
        for f in range(4):
            total = total + colt[0:LONS, 4 * a + f : 4 * a + f + 1] * embed_ref[f : f + 1, :]
        drv[a + 3, 0:LONS, 0:OC] = total.astype(BF16)

    lat_low = pltpu.make_async_remote_copy(
        src_ref=drv.at[pl.ds(12, 3)], dst_ref=drv.at[pl.ds(0, 3)], send_sem=h_send.at[0],
        recv_sem=h_recv.at[0], device_id=lat_dev(1), device_id_type=MESH,
    )
    lat_high = pltpu.make_async_remote_copy(
        src_ref=drv.at[pl.ds(3, 3)], dst_ref=drv.at[pl.ds(15, 3)], send_sem=h_send.at[1],
        recv_sem=h_recv.at[1], device_id=lat_dev(-1), device_id_type=MESH,
    )
    lat_low.start()
    lat_high.start()

    sgs[...] = jnp.zeros_like(sgs)
    sgs[0:CB] = sgain_ref[...]
    sgs[CB : 2 * CB] = sgain_ref[...]
    sg2[...] = jnp.transpose(sgs[...], (1, 0))
    fws[...] = jnp.zeros_like(fws)
    fws[0:4] = fw_ref[...].astype(F32)
    fwt = fws[...].astype(BF16)
    cker[...] = jnp.zeros_like(cker)
    for i in range(7):
        cker[8 * i : 8 * i + 7, 0:OC] = ck_ref[i]

    slot = 2 * yz + h

    def z_copy(k, j):
        return pltpu.make_async_remote_copy(
            src_ref=spec[k].at[j], dst_ref=rspec[k].at[slot], send_sem=z_send.at[k],
            recv_sem=z_recv.at[k], device_id=mode_dev(j), device_id_type=MESH,
        )

    def z_local(k):
        return pltpu.make_async_copy(spec[k].at[a_id], rspec[k].at[slot], loc_sem.at[2 + k])

    blank = jnp.zeros((8, 128), F32)

    def forward(k):
        width = CHUNKS[k][2]
        if k == 1:
            for s in range(2):
                for n in range(4):
                    gin[s, ROWS * n : ROWS * n + ROWS, 0:128] = got[k][s, n, 0:ROWS, :]
                    tile = got[k][s, n, ROWS:288, :]
                    gin[s, ROWS * n : ROWS * n + 96, 128:256] = tile
                    turned = pltpu.roll(tile.astype(F32), 64, axis=1).astype(BF16)
                    gin[s, ROWS * n + 96 : ROWS * n + ROWS, 128:256] = turned

        def rhs(s):
            return gin[s] if k == 1 else got[k][s].reshape(4 * ROWS, width)

        def step(i, carry):
            yb = lax.rem(y0 + i, 4)
            lhs = tf[pl.ds(pl.multiple_of(yb * 192, 16), 192), :]
            halves = [
                jnp.dot(lhs, rhs(s), preferred_element_type=F32)
                for s in range(2)
            ]
            for n in range(8):
                part = slice(MODES * n, MODES * n + MODES)
                low, high = halves[0][part], halves[1][part]
                if k == 0:
                    both = jnp.concatenate([low, high], axis=0)
                else:
                    tile = share(low[:, 128:256], high[:, 128:256])
                    both = jnp.concatenate([low[:, 0:128], high[:, 0:128], tile, blank], axis=0)
                spec[k][yb * 8 + n] = both.astype(BF16)

            def send(n, c2):
                j = yb * 8 + lax.rem(2 * z0 + n, 8)
                mine = self_peer & (j == a_id)

                @pl.when(jnp.logical_not(mine))
                def _():
                    z_copy(k, j).start()

                @pl.when(mine)
                def _():
                    z_local(k).start()

                return c2

            lax.fori_loop(0, 8, send, 0)
            return carry

        lax.fori_loop(0, 4, step, 0)

    def peers_all(k, send, recv, act):
        @pl.when(self_peer)
        def _():
            act(covers(rspec[k].at[pl.ds(0, PEERS - 1)], send.at[k], recv.at[k]))

        @pl.when(jnp.logical_not(self_peer))
        def _():
            act(covers(rspec[k], send.at[k], recv.at[k]))

    tf_copy.wait()
    x_wait(1)
    x_start(0)
    forward(1)

    lat_low.wait_recv()
    lat_high.wait_recv()

    @pl.when(a_id == 0)
    def _():
        drv[0:3] = jnp.zeros((3, ROWS, 256), BF16)

    @pl.when(a_id == 31)
    def _():
        drv[15:18] = jnp.zeros((3, ROWS, 256), BF16)

    edge_l[...] = drv[:, 0:16, :]
    edge_r[...] = drv[:, 176:192, :]
    lon_low = pltpu.make_async_remote_copy(
        src_ref=edge_r, dst_ref=halo_l, send_sem=h_send.at[2],
        recv_sem=h_recv.at[2], device_id=lon_dev(1), device_id_type=MESH,
    )
    lon_high = pltpu.make_async_remote_copy(
        src_ref=edge_l, dst_ref=halo_r, send_sem=h_send.at[3],
        recv_sem=h_recv.at[3], device_id=lon_dev(-1), device_id_type=MESH,
    )
    lon_low.start()
    lon_high.start()

    leg_copy.wait()
    new = lax.broadcasted_iota(jnp.int32, (C, C), 0)
    old = lax.broadcasted_iota(jnp.int32, (C, C), 1)
    order = (old == lax.rem(new, 32) * LATS + new // 32).astype(F32).astype(BF16)

    def permute(m, carry):
        table = leg[m]
        leg_p[m] = lax.dot_general(
            table, order, (((1,), (1,)), ((), ())), preferred_element_type=F32
        ).astype(BF16)
        leg_t[m] = lax.dot_general(
            order, table, (((1,), (1,)), ((), ())), preferred_element_type=F32
        ).astype(BF16)
        return carry

    lax.fori_loop(0, LATS, permute, 0)

    x_wait(0)
    forward(0)

    lon_low.wait_recv()
    lon_high.wait_recv()

    def place(r, carry):
        cpad[r, 0:8, :] = pltpu.roll(halo_l[r].astype(F32), 15, axis=0)[0:8]
        cpad[r, 176:192, :] = jnp.zeros((16, 256), F32)
        cpad[r, 183:189, :] = halo_r[r].astype(F32)[0:6]
        cpad[r, 3:183, :] = drv[r, 0:LONS, :].astype(F32)
        return carry

    lax.fori_loop(0, LATS + 6, place, 0)
    lane = lax.broadcasted_iota(jnp.int32, (ROWS, 256), 1)

    def ocean(a, carry):
        halves = []
        for t in range(2):
            part = slice(128 * t, 128 * t + 128)
            total = None
            for j in range(7):
                acc = None
                for i in range(7):
                    term = cker[8 * i + j : 8 * i + j + 1, part] * cpad[a + i, :, part]
                    acc = term if acc is None else acc + term
                if j:
                    acc = pltpu.roll(acc, ROWS - j, axis=0)
                total = acc if total is None else total + acc
            halves.append(total)
        conv = jnp.concatenate(halves, axis=1)
        mean = jnp.sum(conv, axis=1, keepdims=True) * (1.0 / OC)
        centred = jnp.where(lane < OC, conv - mean, 0.0)
        var = jnp.sum(centred * centred, axis=1, keepdims=True) * (1.0 / OC)
        scaled = centred * lax.rsqrt(var + 1e-05)
        normed = (scaled[:, 0:OC] * ngain_ref[...]).astype(BF16)
        hidden = jax.nn.gelu(
            jnp.dot(normed, up_ref[...], preferred_element_type=F32)
        ).astype(BF16)
        update = lax.dot_general(
            hidden, down_ref[...], (((1,), (1,)), ((), ())), preferred_element_type=F32
        )
        mask_lane = lax.broadcasted_iota(jnp.int32, (ROWS, 128), 1)
        sea = jnp.sum(
            jnp.where(mask_lane == 64 + a, colt[0:ROWS, :], 0.0), axis=1, keepdims=True
        )
        held = drv[a + 3, :, 0:OC].astype(F32) + update
        oc_out[a] = jnp.where(sea == 1.0, held, 0.0)[0:LONS].astype(BF16)
        return carry

    lax.fori_loop(0, LATS, ocean, 0)

    def add_halves(k):

        def step(i, carry):
            both = rspec[k][2 * i].astype(F32) + rspec[k][2 * i + 1].astype(F32)
            at = pl.ds(pl.multiple_of(i * 48, 8), 48)
            if k == 0:
                for t in range(3):
                    rsum[t, at, :] = both[:, 128 * t : 128 * t + 128]
            else:
                rsum[3, at, :] = both[0:48]
                tile = both[48:72]
                rsum[4, at, :] = jnp.concatenate([tile, pltpu.roll(tile, 64, axis=1)], axis=0)
            return carry

        lax.fori_loop(0, 16, step, 0)

    def z_wait(k):
        peers_all(k, z_send, z_recv, lambda copy: copy.wait_recv())

        @pl.when(self_peer)
        def _():
            z_local(k).wait()

    spans = ((range(0, 8), 0, 3), (range(8, LATS), 3, 5))

    def gather(k, m):
        bands, first, end = spans[k]
        rows = {
            (p, t): rsum[t, pl.ds(2 * m + p, 32, stride=MODES), :]
            for p in range(2)
            for t in range(first, end)
        }
        blocks = []
        for a in bands:
            moves = [(p, CB * a, CB * p, CB) for p in range(2)]
            blocks.append(move_lanes(moves, 1, lambda key, t: rows[key, t], 32)[0])
        return jnp.concatenate(blocks, axis=0).astype(BF16)

    def scatter(k, m, synth):
        bands, first, end = spans[k]
        for p in range(2):
            moves = [(n, CB * p, CB * a - 128 * first, CB) for n, a in enumerate(bands)]
            tiles = move_lanes(
                moves, end - first, lambda key, t: synth[32 * key : 32 * key + 32], 32
            )
            for t, value in enumerate(tiles):
                ssum[first + t, pl.ds(2 * m + p, 32, stride=MODES), :] = value

    def each_mode(work):
        def go(i, carry):
            for n in range(3):
                work(3 * i + n)
            return carry

        lax.fori_loop(0, LATS // 3, go, 0)

    def early(m):
        coef[m] = jnp.dot(leg_p[m, :, 256:384], gather(1, m), preferred_element_type=F32)

    def middle(m):
        coeffs = coef[m] + jnp.dot(leg_p[m, :, 0:256], gather(0, m), preferred_element_type=F32)
        filtered = (coeffs * sg2[...]).astype(BF16)
        filt[m] = filtered
        scatter(0, m, jnp.dot(leg_t[m, 0:256, :], filtered, preferred_element_type=F32))

    def late(m):
        scatter(1, m, jnp.dot(leg_t[m, 256:384, :], filt[m], preferred_element_type=F32))

    z_wait(1)
    add_halves(1)
    each_mode(early)
    z_wait(0)
    add_halves(0)
    each_mode(middle)

    def zi_copy(k, j):
        return pltpu.make_async_remote_copy(
            src_ref=syn[k].at[j // 2], dst_ref=rsyn[k].at[a_id], send_sem=zi_send.at[k],
            recv_sem=zi_recv.at[k], device_id=band_dev(j), device_id_type=MESH,
        )

    def zi_local(k):
        return pltpu.make_async_copy(syn[k].at[yz], rsyn[k].at[a_id], loc_sem.at[4 + k])

    def back(k, fill, send):
        def step(i, carry):
            b = lax.rem(y0 + i // 4, 4) * 4 + lax.rem(z0 + i, 4)
            at = pl.ds(pl.multiple_of(b * 48, 8), 48)
            if fill and k == 0:
                for t in range(3):
                    syn[k][b, :, 128 * t : 128 * t + 128] = ssum[t, at, :].astype(BF16)
            elif fill:
                last = ssum[4, at, :]
                tile = share(last[0:MODES], last[MODES:48])
                both = jnp.concatenate([ssum[3, at, :], tile, blank], axis=0)
                syn[k][b] = both.astype(BF16)
            for n in range(2 if send else 0):
                j = 2 * b + n
                mine = self_peer & (j == 2 * yz + h)

                @pl.when(jnp.logical_not(mine))
                def _():
                    zi_copy(k, j).start()

                @pl.when(mine)
                def _():
                    zi_local(k).start()

            return carry

        lax.fori_loop(0, 16, step, 0)

    back(0, True, True)
    each_mode(late)
    back(1, True, False)
    peers_all(0, zi_send, zi_recv, lambda copy: copy.wait_send())
    back(1, False, True)

    def zi_wait(k):
        peers_all(k, zi_send, zi_recv, lambda copy: copy.wait_recv())

        @pl.when(self_peer)
        def _():
            zi_local(k).wait()

    def xi_copy(k, q):
        return pltpu.make_async_remote_copy(
            src_ref=gs[k].at[q], dst_ref=rg[k].at[me], send_sem=xi_send.at[k],
            recv_sem=xi_recv.at[k], device_id=row_dev(q), device_id_type=MESH,
        )

    def xi_local(k):
        return pltpu.make_async_copy(gs[k].at[me], rg[k].at[me], loc_sem.at[6 + k])

    def inverse(k):
        def regroup(i, carry):
            first = rsyn[k][2 * i].astype(F32)
            second = rsyn[k][2 * i + 1].astype(F32)
            for s in range(2):
                part = slice(MODES * s, MODES * s + MODES)
                at = pl.ds(pl.multiple_of(i * 48, 16), 48)
                both = jnp.concatenate([first[part], second[part]], axis=0)
                if k == 0:
                    sy[k][s, at, :] = both.astype(BF16)
                else:
                    sy[k][s, at, 0:128] = both.astype(BF16)
                    both = jnp.concatenate([first[48:72], second[48:72]], axis=0)
                    if s:
                        both = pltpu.roll(both, 64, axis=1)
                    sy[k][s, at, 128:256] = both.astype(BF16)
            return carry

        lax.fori_loop(0, 16, regroup, 0)

        def step(i, carry):
            xb = lax.rem(x + i, 4)
            lhs = ti[pl.ds(pl.multiple_of(xb * ROWS, 16), ROWS), :]
            for s in range(2):
                q = 2 * xb + s
                values = jnp.dot(lhs, sy[k][s], preferred_element_type=F32)
                if k == 1:
                    tile = share(values[0:96, 128:256], values[96:ROWS, 128:256])
                    values = jnp.concatenate([values[:, 0:128], tile], axis=0)
                gs[k][q] = values.astype(BF16)

                @pl.when(q != me)
                def _():
                    xi_copy(k, q).start()

                @pl.when(q == me)
                def _():
                    xi_local(k).start()

            return carry

        lax.fori_loop(0, 4, step, 0)

    def xi_wait(k):
        x_all(k, xi_send, xi_recv).wait_recv()
        xi_local(k).wait()

    def finish(k):
        a0, na, width = CHUNKS[k]

        def came(q, t):
            if k == 0:
                return rg[k][q, :, 128 * t : 128 * t + 128].astype(F32)
            if t == 0:
                return rg[k][q, 0:ROWS, :].astype(F32)
            tile = rg[k][q, ROWS:288, :].astype(F32)
            return jnp.concatenate([tile, pltpu.roll(tile, 64, axis=1)], axis=0)

        for a in range(na):
            moves = [(q, CB * a, CB * q, CB) for q in range(8)]
            tiles = move_lanes(moves, 3, came, ROWS)
            grid = jnp.concatenate(tiles, axis=1)
            mixed = forced[a0 + a].astype(F32) + grid
            active = jax.nn.gelu(mixed).astype(BF16)
            result = mixed + jnp.dot(active, mix_ref[...], preferred_element_type=F32)
            result = result.astype(BF16)
            atm_out[a0 + a] = result[0:LONS]
            fluxes = lax.dot_general(
                fwt, result, (((1,), (1,)), ((), ())), preferred_element_type=F32
            )
            flux_out[a0 + a] = fluxes[0:4, 0:LONS]

    ti_copy.wait()
    zi_wait(0)
    inverse(0)
    zi_wait(1)
    inverse(1)
    xi_wait(0)
    finish(0)
    xi_wait(1)
    finish(1)

    for k in range(2):
        x_all(k, x_send, x_recv).wait_send()
        x_all(k, xi_send, xi_recv).wait_send()
        peers_all(k, z_send, z_recv, lambda copy: copy.wait_send())
    peers_all(1, zi_send, zi_recv, lambda copy: copy.wait_send())
    for copy in (lat_low, lat_high, lon_low, lon_high):
        copy.wait_send()


def local(
    atmosphere, ocean_state, surface_flux, land_sea, surface_read, surface_gain, legendre,
    spectral_gain, mixing, flux_weight, flux_embed, conv_kernel, norm_gain, ocean_up, ocean_down,
):
    forward_table, inverse_table = lon_tables()
    vm = pl.BlockSpec(memory_space=pltpu.VMEM)
    hbm = pl.BlockSpec(memory_space=pl.ANY)
    wide = [w for _, _, w in CHUNKS]

    def pair(*dims):
        return [pltpu.VMEM(dims + (w,), BF16) for w in wide]

    def message(count):
        return [pltpu.VMEM((count, 48, 384), BF16), pltpu.VMEM((count, 80, 128), BF16)]

    def crossing(*dims):
        return [pltpu.VMEM(dims + (ROWS, 384), BF16), pltpu.VMEM(dims + (288, 128), BF16)]

    dma = pltpu.SemaphoreType.DMA
    atm_next, flux_next, ocean_next = pl.pallas_call(
        body,
        out_shape=(
            jax.ShapeDtypeStruct((LATS, LONS, C), BF16),
            jax.ShapeDtypeStruct((LATS, 4, LONS), F32),
            jax.ShapeDtypeStruct((LATS, LONS, OC), BF16),
        ),
        in_specs=[vm] * 6 + [hbm] + [vm] * 8 + [hbm] * 2,
        out_specs=(vm, vm, vm),
        scratch_shapes=[
            pltpu.VMEM((2 * M, 4 * ROWS), BF16),
            pltpu.VMEM((4 * ROWS, 2 * M), BF16),
            pltpu.VMEM((LATS, C, C), BF16),
            pltpu.VMEM((LATS, C, C), BF16),
            pltpu.VMEM((LATS, C, C), BF16),
            pltpu.VMEM((LATS, ROWS, C), BF16),
            *crossing(8),
            *crossing(2, 4),
            pltpu.VMEM((2, 4 * ROWS, 256), BF16),
            *message(PEERS),
            *message(PEERS),
            pltpu.VMEM((5, 768, 128), F32),
            pltpu.VMEM((5, 768, 128), F32),
            *message(16),
            *message(PEERS),
            *pair(2, 768),
            *crossing(8),
            *crossing(8),
            pltpu.VMEM((LATS, C, 128), F32),
            pltpu.VMEM((LATS, C, 128), BF16),
            pltpu.VMEM((128, C), F32),
            pltpu.VMEM((C, 128), F32),
            pltpu.VMEM((128, 256), F32),
            pltpu.VMEM((256, 128), F32),
            pltpu.VMEM((16, C), F32),
            pltpu.VMEM((LATS + 6, ROWS, 256), BF16),
            pltpu.VMEM((LATS + 6, 16, 256), BF16),
            pltpu.VMEM((LATS + 6, 16, 256), BF16),
            pltpu.VMEM((LATS + 6, 16, 256), BF16),
            pltpu.VMEM((LATS + 6, 16, 256), BF16),
            pltpu.VMEM((LATS + 6, ROWS, 256), F32),
            pltpu.VMEM((56, 256), F32),
            dma((3,)), dma((2,)), dma((2,)), dma((2,)), dma((2,)), dma((2,)), dma((2,)),
            dma((2,)), dma((2,)), dma((4,)), dma((4,)), dma((8,)),
        ],
        compiler_params=pltpu.CompilerParams(
            collective_id=0, has_side_effects=True, vmem_limit_bytes=VMEM_LIMIT
        ),
        name="window",
    )(
        atmosphere, ocean_state,
        jnp.transpose(surface_flux, (1, 0, 2)), land_sea, surface_read,
        surface_gain.reshape(3, 128), legendre, spectral_gain.T, mixing, flux_weight.T, flux_embed,
        conv_kernel, norm_gain.reshape(1, OC), ocean_up, ocean_down.T,
        jnp.asarray(forward_table), jnp.asarray(inverse_table),
    )
    return atm_next, jnp.transpose(flux_next, (1, 0, 2)), ocean_next


def solution(mesh):
    grid = P("atm", ("ocn", "ch"), None)
    return jax.shard_map(
        local,
        mesh=mesh,
        in_specs=(
            grid, grid, P(None, "atm", ("ocn", "ch")), P("atm", ("ocn", "ch")), P(), P(),
            P("atm", None, None), P(None, ("ocn", "ch")), P(), P(), P(), P(), P(), P(), P(),
        ),
        out_specs=(grid, P(None, "atm", ("ocn", "ch")), grid),
        check_vma=False,
    )
```

```python
import math

import jax
import jax.numpy as jnp
import ml_dtypes
import numpy as np
from jax import lax
from jax.experimental import pallas as pl
from jax.experimental.pallas import tpu as pltpu
from jax.sharding import PartitionSpec as P

M = 384
NLON = 1440
C = 384
OC = 200
HID = 800
LATS = 12
LONS = 180
ROWS = 192
CB = 48
PEERS = 32
MODES = 24
CHUNKS = ((0, 8, 384), (8, 4, 256))
MESH = pl.DeviceIdType.MESH
F32 = jnp.float32
BF16 = jnp.bfloat16
VMEM_LIMIT = 60 * 2**20


def lon_tables():
    lon = np.arange(NLON, dtype=np.int64)
    wave = np.arange(M, dtype=np.int64)
    phase = (lon[:, None] * wave[None, :]) % NLON
    angle = phase.astype(np.float32) * np.float32(2.0 * math.pi / NLON)
    table = np.stack([np.cos(angle), -np.sin(angle)], axis=2) * np.float32(NLON**-0.5)
    table = table.astype(np.float32).reshape(4, 2, LONS, 2 * M).transpose(1, 0, 2, 3)
    padded = np.zeros((2, 4, ROWS, 2 * M), np.float32)
    padded[:, :, :LONS] = table
    inverse = padded.reshape(2, 4 * ROWS, 2 * M).astype(ml_dtypes.bfloat16)
    return np.ascontiguousarray(inverse.transpose(0, 2, 1)), inverse


def segments(src, dst, count):
    out = []
    done = 0
    while done < count:
        s, d = src + done, dst + done
        step = min(count - done, 128 - s % 128, 128 - d % 128)
        out.append((s // 128, d // 128, (d - s) % 128, d % 128, d % 128 + step))
        done += step
    return out


def move_lanes(moves, tiles, get, rows):
    lane = lax.broadcasted_iota(jnp.int32, (rows, 128), 1)
    out = [None] * tiles
    for key, src, dst, count in moves:
        for s_tile, d_tile, shift, low, high in segments(src, dst, count):
            piece = get(key, s_tile)
            if shift:
                piece = pltpu.roll(piece, shift, axis=1)
            if out[d_tile] is None:
                if low == 0:
                    out[d_tile] = jnp.where(lane < high, piece, 0.0)
                else:
                    out[d_tile] = jnp.where((lane >= low) & (lane < high), piece, 0.0)
            else:
                out[d_tile] = jnp.where((lane >= low) & (lane < high), piece, out[d_tile])
    return out


def body(
    atm_ref, oc_ref, flux_ref, land_ref, read_ref, gain_ref, leg_hbm, sgain_ref, mix_ref, fw_ref,
    embed_ref, ck_ref, ngain_ref, up_ref, down_ref, tf_hbm, ti_hbm,
    atm_out, flux_out, oc_out,
    tf, ti, leg, leg_p, leg_t, forced,
    pack_a, pack_b, got_a, got_b, gin, spec_a, spec_b, rspec_a, rspec_b, rsum, ssum,
    syn_a, syn_b, rsyn_a, rsyn_b, sy_a, sy_b, gs_a, gs_b, rg_a, rg_b,
    coef, filt, sgs, sg2, cols, colt, fws, drv, edge_l, edge_r, halo_l, halo_r, cpad, cker,
    in_sem, x_send, x_recv, z_send, z_recv, zi_send, zi_recv, xi_send, xi_recv, h_send, h_recv, loc_sem,
):
    pack, got, spec, rspec = (pack_a, pack_b), (got_a, got_b), (spec_a, spec_b), (rspec_a, rspec_b)
    syn, rsyn, sy, gs, rg = (syn_a, syn_b), (rsyn_a, rsyn_b), (sy_a, sy_b), (gs_a, gs_b), (rg_a, rg_b)
    a_id = lax.axis_index("atm")
    x = lax.axis_index("ocn")
    h = lax.axis_index("ch")
    core = lax.rem(a_id, 2)
    yz = a_id // 2
    y0 = yz // 4
    z0 = lax.rem(yz, 4)
    me = 2 * x + core
    lon_block = 2 * x + h
    self_peer = core == h
    n_remote = PEERS - self_peer.astype(jnp.int32)

    tf_copy = pltpu.make_async_copy(tf_hbm.at[h], tf, in_sem.at[0])
    ti_copy = pltpu.make_async_copy(ti_hbm.at[h], ti, in_sem.at[1])
    leg_copy = pltpu.make_async_copy(leg_hbm, leg, in_sem.at[2])
    tf_copy.start()
    leg_copy.start()
    ti_copy.start()

    def row_dev(q):
        return {"atm": 2 * yz + lax.rem(q, 2), "ocn": q // 2, "ch": h}

    def mode_dev(j):
        return {"atm": j, "ocn": x, "ch": core}

    def band_dev(j):
        return {"atm": (j // 2) * 2 + h, "ocn": x, "ch": lax.rem(j, 2)}

    def lat_dev(step):
        return {"atm": lax.rem(a_id + step + 32, 32), "ocn": x, "ch": h}

    def lon_dev(step):
        b = lax.rem(lon_block + step + 8, 8)
        return {"atm": a_id, "ocn": b // 2, "ch": lax.rem(b, 2)}

    barrier = pltpu.get_barrier_semaphore()

    def greet(device):
        pl.semaphore_signal(barrier, inc=1, device_id=device, device_id_type=MESH)

    def greet_row(i, carry):
        greet(row_dev(lax.rem(me + i, 8)))
        return carry

    lax.fori_loop(1, 8, greet_row, 0)
    for step in (-1, 1):
        greet(lat_dev(step))
        greet(lon_dev(step))

    def greet_peers(j, carry):
        @pl.when(jnp.logical_not(self_peer & (j == a_id)))
        def _():
            greet(mode_dev(j))

        @pl.when(jnp.logical_not(self_peer & (j == 2 * yz + h)))
        def _():
            greet(band_dev(j))

        return carry

    lax.fori_loop(0, PEERS, greet_peers, 0)

    forced[:, 176:192, :] = jnp.zeros((LATS, 16, C), BF16)

    read_row = read_ref[...].astype(F32).reshape(1, OC)

    def force(a, carry):
        seen = oc_ref[a].astype(F32) * read_row
        surface = jnp.sum(seen, axis=1, keepdims=True)
        for t in range(3):
            part = slice(128 * t, 128 * t + 128)
            total = atm_ref[a, :, part].astype(F32) + surface * gain_ref[t : t + 1, :]
            forced[a, 0:LONS, part] = total.astype(BF16)
        return carry

    lax.fori_loop(CHUNKS[1][0], LATS, force, 0)

    def share(low, high):
        lanes = lax.broadcasted_iota(jnp.int32, low.shape, 1)
        return jnp.where(lanes < 64, low, pltpu.roll(high, 64, axis=1))

    def pack_chunk(k):
        a0, na, width = CHUNKS[k]

        def pieces(r0):
            held = {}
            for a in range(na):
                for t in range(3):
                    held[a, t] = forced[a0 + a, pl.ds(r0, 48), 128 * t : 128 * t + 128].astype(F32)
            for q in range(8):
                moves = [(a, CB * q, CB * a, CB) for a in range(na)]
                yield q, move_lanes(moves, width // 128, lambda key, t: held[key, t], 48)

        def whole_step(rb, carry):
            r0 = pl.multiple_of(rb * 48, 16)
            for q, tiles in pieces(r0):
                for t, value in enumerate(tiles):
                    pack[k][q, pl.ds(r0, 48), 128 * t : 128 * t + 128] = value.astype(BF16)
            return carry

        def shared_step(rb, carry):
            r0 = pl.multiple_of(rb * 48, 16)
            r1 = pl.multiple_of(rb * 48 + 96, 16)
            r2 = pl.multiple_of(rb * 48 + ROWS, 16)
            for (q, low), (_, high) in zip(pieces(r0), pieces(r1)):
                pack[k][q, pl.ds(r0, 48), :] = low[0].astype(BF16)
                pack[k][q, pl.ds(r1, 48), :] = high[0].astype(BF16)
                pack[k][q, pl.ds(r2, 48), :] = share(low[1], high[1]).astype(BF16)
            return carry

        if k == 0:
            lax.fori_loop(0, 4, whole_step, 0)
        else:
            lax.fori_loop(0, 2, shared_step, 0)

    def x_copy(k, q):
        return pltpu.make_async_remote_copy(
            src_ref=pack[k].at[q], dst_ref=got[k].at[core, x], send_sem=x_send.at[k],
            recv_sem=x_recv.at[k], device_id=row_dev(q), device_id_type=MESH,
        )

    def x_start(k):
        pltpu.make_async_copy(pack[k].at[me], got[k].at[core, x], loc_sem.at[k]).start()

        def go(i, carry):
            x_copy(k, lax.rem(me + i, 8)).start()
            return carry

        lax.fori_loop(1, 8, go, 0)

    def covers(ref, send, recv):
        return pltpu.make_async_remote_copy(
            src_ref=ref, dst_ref=ref, send_sem=send, recv_sem=recv,
            device_id=lat_dev(1), device_id_type=MESH,
        )

    def x_all(k, send, recv):
        return covers(pack[k].at[pl.ds(0, 7)], send.at[k], recv.at[k])

    def x_wait(k):
        pltpu.make_async_copy(pack[k].at[me], got[k].at[core, x], loc_sem.at[k]).wait()
        x_all(k, x_send, x_recv).wait_recv()

    pack_chunk(1)
    pl.semaphore_wait(barrier, 2 * n_remote + 7 + 4)
    x_start(1)
    lax.fori_loop(0, CHUNKS[1][0], force, 0)
    pack_chunk(0)

    cols[...] = jnp.zeros_like(cols)
    for a in range(LATS):
        cols[4 * a : 4 * a + 4, 0:LONS] = flux_ref[a]
    cols[64 : 64 + LATS, 0:LONS] = land_ref[...].astype(F32)
    colt[...] = jnp.transpose(cols[...], (1, 0))
    drv[3:15, 176:192, :] = jnp.zeros((LATS, 16, 256), BF16)
    drv[3:15, :, 128:256] = jnp.zeros((LATS, ROWS, 128), BF16)
    for a in range(LATS):
        total = oc_ref[a].astype(F32)
        for f in range(4):
            total = total + colt[0:LONS, 4 * a + f : 4 * a + f + 1] * embed_ref[f : f + 1, :]
        drv[a + 3, 0:LONS, 0:OC] = total.astype(BF16)

    lat_low = pltpu.make_async_remote_copy(
        src_ref=drv.at[pl.ds(12, 3)], dst_ref=drv.at[pl.ds(0, 3)], send_sem=h_send.at[0],
        recv_sem=h_recv.at[0], device_id=lat_dev(1), device_id_type=MESH,
    )
    lat_high = pltpu.make_async_remote_copy(
        src_ref=drv.at[pl.ds(3, 3)], dst_ref=drv.at[pl.ds(15, 3)], send_sem=h_send.at[1],
        recv_sem=h_recv.at[1], device_id=lat_dev(-1), device_id_type=MESH,
    )
    lat_low.start()
    lat_high.start()

    sgs[...] = jnp.zeros_like(sgs)
    sgs[0:CB] = sgain_ref[...]
    sgs[CB : 2 * CB] = sgain_ref[...]
    sg2[...] = jnp.transpose(sgs[...], (1, 0))
    fws[...] = jnp.zeros_like(fws)
    fws[0:4] = fw_ref[...].astype(F32)
    fwt = fws[...].astype(BF16)
    cker[...] = jnp.zeros_like(cker)
    for i in range(7):
        cker[8 * i : 8 * i + 7, 0:OC] = ck_ref[i]

    slot = 2 * yz + h

    def z_copy(k, j):
        return pltpu.make_async_remote_copy(
            src_ref=spec[k].at[j], dst_ref=rspec[k].at[slot], send_sem=z_send.at[k],
            recv_sem=z_recv.at[k], device_id=mode_dev(j), device_id_type=MESH,
        )

    def z_local(k):
        return pltpu.make_async_copy(spec[k].at[a_id], rspec[k].at[slot], loc_sem.at[2 + k])

    blank = jnp.zeros((8, 128), F32)

    def forward(k):
        width = CHUNKS[k][2]
        if k == 1:
            for s in range(2):
                for n in range(4):
                    gin[s, ROWS * n : ROWS * n + ROWS, 0:128] = got[k][s, n, 0:ROWS, :]
                    tile = got[k][s, n, ROWS:288, :]
                    gin[s, ROWS * n : ROWS * n + 96, 128:256] = tile
                    turned = pltpu.roll(tile.astype(F32), 64, axis=1).astype(BF16)
                    gin[s, ROWS * n + 96 : ROWS * n + ROWS, 128:256] = turned

        def rhs(s):
            return gin[s] if k == 1 else got[k][s].reshape(4 * ROWS, width)

        def step(i, carry):
            yb = lax.rem(y0 + i, 4)
            lhs = tf[pl.ds(pl.multiple_of(yb * 192, 16), 192), :]
            halves = [
                jnp.dot(lhs, rhs(s), preferred_element_type=F32)
                for s in range(2)
            ]
            for n in range(8):
                part = slice(MODES * n, MODES * n + MODES)
                low, high = halves[0][part], halves[1][part]
                if k == 0:
                    both = jnp.concatenate([low, high], axis=0)
                else:
                    tile = share(low[:, 128:256], high[:, 128:256])
                    both = jnp.concatenate([low[:, 0:128], high[:, 0:128], tile, blank], axis=0)
                spec[k][yb * 8 + n] = both.astype(BF16)

            def send(n, c2):
                j = yb * 8 + lax.rem(2 * z0 + n, 8)
                mine = self_peer & (j == a_id)

                @pl.when(jnp.logical_not(mine))
                def _():
                    z_copy(k, j).start()

                @pl.when(mine)
                def _():
                    z_local(k).start()

                return c2

            lax.fori_loop(0, 8, send, 0)
            return carry

        lax.fori_loop(0, 4, step, 0)

    def peers_all(k, send, recv, act):
        @pl.when(self_peer)
        def _():
            act(covers(rspec[k].at[pl.ds(0, PEERS - 1)], send.at[k], recv.at[k]))

        @pl.when(jnp.logical_not(self_peer))
        def _():
            act(covers(rspec[k], send.at[k], recv.at[k]))

    tf_copy.wait()
    x_wait(1)
    x_start(0)
    forward(1)

    lat_low.wait_recv()
    lat_high.wait_recv()

    @pl.when(a_id == 0)
    def _():
        drv[0:3] = jnp.zeros((3, ROWS, 256), BF16)

    @pl.when(a_id == 31)
    def _():
        drv[15:18] = jnp.zeros((3, ROWS, 256), BF16)

    edge_l[...] = drv[:, 0:16, :]
    edge_r[...] = drv[:, 176:192, :]
    lon_low = pltpu.make_async_remote_copy(
        src_ref=edge_r, dst_ref=halo_l, send_sem=h_send.at[2],
        recv_sem=h_recv.at[2], device_id=lon_dev(1), device_id_type=MESH,
    )
    lon_high = pltpu.make_async_remote_copy(
        src_ref=edge_l, dst_ref=halo_r, send_sem=h_send.at[3],
        recv_sem=h_recv.at[3], device_id=lon_dev(-1), device_id_type=MESH,
    )
    lon_low.start()
    lon_high.start()

    leg_copy.wait()
    new = lax.broadcasted_iota(jnp.int32, (C, C), 0)
    old = lax.broadcasted_iota(jnp.int32, (C, C), 1)
    order = (old == lax.rem(new, 32) * LATS + new // 32).astype(F32).astype(BF16)

    def permute(m, carry):
        table = leg[m]
        leg_p[m] = lax.dot_general(
            table, order, (((1,), (1,)), ((), ())), preferred_element_type=F32
        ).astype(BF16)
        leg_t[m] = lax.dot_general(
            order, table, (((1,), (1,)), ((), ())), preferred_element_type=F32
        ).astype(BF16)
        return carry

    lax.fori_loop(0, LATS, permute, 0)

    x_wait(0)
    forward(0)

    lon_low.wait_recv()
    lon_high.wait_recv()

    def place(r, carry):
        cpad[r, 0:8, :] = pltpu.roll(halo_l[r].astype(F32), 15, axis=0)[0:8]
        cpad[r, 176:192, :] = jnp.zeros((16, 256), F32)
        cpad[r, 183:189, :] = halo_r[r].astype(F32)[0:6]
        cpad[r, 3:183, :] = drv[r, 0:LONS, :].astype(F32)
        return carry

    lax.fori_loop(0, LATS + 6, place, 0)
    lane = lax.broadcasted_iota(jnp.int32, (ROWS, 256), 1)

    def ocean(a, carry):
        halves = []
        for t in range(2):
            part = slice(128 * t, 128 * t + 128)
            total = None
            for j in range(7):
                acc = None
                for i in range(7):
                    term = cker[8 * i + j : 8 * i + j + 1, part] * cpad[a + i, :, part]
                    acc = term if acc is None else acc + term
                if j:
                    acc = pltpu.roll(acc, ROWS - j, axis=0)
                total = acc if total is None else total + acc
            halves.append(total)
        conv = jnp.concatenate(halves, axis=1)
        mean = jnp.sum(conv, axis=1, keepdims=True) * (1.0 / OC)
        centred = jnp.where(lane < OC, conv - mean, 0.0)
        var = jnp.sum(centred * centred, axis=1, keepdims=True) * (1.0 / OC)
        scaled = centred * lax.rsqrt(var + 1e-05)
        normed = (scaled[:, 0:OC] * ngain_ref[...]).astype(BF16)
        hidden = jax.nn.gelu(
            jnp.dot(normed, up_ref[...], preferred_element_type=F32)
        ).astype(BF16)
        update = lax.dot_general(
            hidden, down_ref[...], (((1,), (1,)), ((), ())), preferred_element_type=F32
        )
        mask_lane = lax.broadcasted_iota(jnp.int32, (ROWS, 128), 1)
        sea = jnp.sum(
            jnp.where(mask_lane == 64 + a, colt[0:ROWS, :], 0.0), axis=1, keepdims=True
        )
        held = drv[a + 3, :, 0:OC].astype(F32) + update
        oc_out[a] = jnp.where(sea == 1.0, held, 0.0)[0:LONS].astype(BF16)
        return carry

    lax.fori_loop(0, LATS, ocean, 0)

    def add_halves(k):

        def step(i, carry):
            both = rspec[k][2 * i].astype(F32) + rspec[k][2 * i + 1].astype(F32)
            at = pl.ds(pl.multiple_of(i * 48, 8), 48)
            if k == 0:
                for t in range(3):
                    rsum[t, at, :] = both[:, 128 * t : 128 * t + 128]
            else:
                rsum[3, at, :] = both[0:48]
                tile = both[48:72]
                rsum[4, at, :] = jnp.concatenate([tile, pltpu.roll(tile, 64, axis=1)], axis=0)
            return carry

        lax.fori_loop(0, 16, step, 0)

    def z_wait(k):
        peers_all(k, z_send, z_recv, lambda copy: copy.wait_recv())

        @pl.when(self_peer)
        def _():
            z_local(k).wait()

    spans = ((range(0, 8), 0, 3), (range(8, LATS), 3, 5))

    def gather(k, m):
        bands, first, end = spans[k]
        rows = {
            (p, t): rsum[t, pl.ds(2 * m + p, 32, stride=MODES), :]
            for p in range(2)
            for t in range(first, end)
        }
        blocks = []
        for a in bands:
            moves = [(p, CB * a, CB * p, CB) for p in range(2)]
            blocks.append(move_lanes(moves, 1, lambda key, t: rows[key, t], 32)[0])
        return jnp.concatenate(blocks, axis=0).astype(BF16)

    def scatter(k, m, synth):
        bands, first, end = spans[k]
        for p in range(2):
            moves = [(n, CB * p, CB * a - 128 * first, CB) for n, a in enumerate(bands)]
            tiles = move_lanes(
                moves, end - first, lambda key, t: synth[32 * key : 32 * key + 32], 32
            )
            for t, value in enumerate(tiles):
                ssum[first + t, pl.ds(2 * m + p, 32, stride=MODES), :] = value

    def each_mode(work):
        def go(i, carry):
            for n in range(3):
                work(3 * i + n)
            return carry

        lax.fori_loop(0, LATS // 3, go, 0)

    def early(m):
        coef[m] = jnp.dot(leg_p[m, :, 256:384], gather(1, m), preferred_element_type=F32)

    def middle(m):
        coeffs = coef[m] + jnp.dot(leg_p[m, :, 0:256], gather(0, m), preferred_element_type=F32)
        filtered = (coeffs * sg2[...]).astype(BF16)
        filt[m] = filtered
        scatter(0, m, jnp.dot(leg_t[m, 0:256, :], filtered, preferred_element_type=F32))

    def late(m):
        scatter(1, m, jnp.dot(leg_t[m, 256:384, :], filt[m], preferred_element_type=F32))

    z_wait(1)
    add_halves(1)
    each_mode(early)
    z_wait(0)
    add_halves(0)
    each_mode(middle)

    def zi_copy(k, j):
        return pltpu.make_async_remote_copy(
            src_ref=syn[k].at[j // 2], dst_ref=rsyn[k].at[a_id], send_sem=zi_send.at[k],
            recv_sem=zi_recv.at[k], device_id=band_dev(j), device_id_type=MESH,
        )

    def zi_local(k):
        return pltpu.make_async_copy(syn[k].at[yz], rsyn[k].at[a_id], loc_sem.at[4 + k])

    def back(k, fill, send):
        def step(i, carry):
            b = lax.rem(y0 + i // 4, 4) * 4 + lax.rem(z0 + i, 4)
            at = pl.ds(pl.multiple_of(b * 48, 8), 48)
            if fill and k == 0:
                for t in range(3):
                    syn[k][b, :, 128 * t : 128 * t + 128] = ssum[t, at, :].astype(BF16)
            elif fill:
                last = ssum[4, at, :]
                tile = share(last[0:MODES], last[MODES:48])
                both = jnp.concatenate([ssum[3, at, :], tile, blank], axis=0)
                syn[k][b] = both.astype(BF16)
            for n in range(2 if send else 0):
                j = 2 * b + n
                mine = self_peer & (j == 2 * yz + h)

                @pl.when(jnp.logical_not(mine))
                def _():
                    zi_copy(k, j).start()

                @pl.when(mine)
                def _():
                    zi_local(k).start()

            return carry

        lax.fori_loop(0, 16, step, 0)

    back(0, True, True)
    each_mode(late)
    back(1, True, False)
    peers_all(0, zi_send, zi_recv, lambda copy: copy.wait_send())
    back(1, False, True)

    def zi_wait(k):
        peers_all(k, zi_send, zi_recv, lambda copy: copy.wait_recv())

        @pl.when(self_peer)
        def _():
            zi_local(k).wait()

    def xi_copy(k, q):
        return pltpu.make_async_remote_copy(
            src_ref=gs[k].at[q], dst_ref=rg[k].at[me], send_sem=xi_send.at[k],
            recv_sem=xi_recv.at[k], device_id=row_dev(q), device_id_type=MESH,
        )

    def xi_local(k):
        return pltpu.make_async_copy(gs[k].at[me], rg[k].at[me], loc_sem.at[6 + k])

    def inverse(k):
        def regroup(i, carry):
            first = rsyn[k][2 * i].astype(F32)
            second = rsyn[k][2 * i + 1].astype(F32)
            for s in range(2):
                part = slice(MODES * s, MODES * s + MODES)
                at = pl.ds(pl.multiple_of(i * 48, 16), 48)
                both = jnp.concatenate([first[part], second[part]], axis=0)
                if k == 0:
                    sy[k][s, at, :] = both.astype(BF16)
                else:
                    sy[k][s, at, 0:128] = both.astype(BF16)
                    both = jnp.concatenate([first[48:72], second[48:72]], axis=0)
                    if s:
                        both = pltpu.roll(both, 64, axis=1)
                    sy[k][s, at, 128:256] = both.astype(BF16)
            return carry

        lax.fori_loop(0, 16, regroup, 0)

        def step(i, carry):
            xb = lax.rem(x + i, 4)
            lhs = ti[pl.ds(pl.multiple_of(xb * ROWS, 16), ROWS), :]
            for s in range(2):
                q = 2 * xb + s
                values = jnp.dot(lhs, sy[k][s], preferred_element_type=F32)
                if k == 1:
                    tile = share(values[0:96, 128:256], values[96:ROWS, 128:256])
                    values = jnp.concatenate([values[:, 0:128], tile], axis=0)
                gs[k][q] = values.astype(BF16)

                @pl.when(q != me)
                def _():
                    xi_copy(k, q).start()

                @pl.when(q == me)
                def _():
                    xi_local(k).start()

            return carry

        lax.fori_loop(0, 4, step, 0)

    def xi_wait(k):
        x_all(k, xi_send, xi_recv).wait_recv()
        xi_local(k).wait()

    def finish(k):
        a0, na, width = CHUNKS[k]

        def came(q, t):
            if k == 0:
                return rg[k][q, :, 128 * t : 128 * t + 128].astype(F32)
            if t == 0:
                return rg[k][q, 0:ROWS, :].astype(F32)
            tile = rg[k][q, ROWS:288, :].astype(F32)
            return jnp.concatenate([tile, pltpu.roll(tile, 64, axis=1)], axis=0)

        for a in range(na):
            moves = [(q, CB * a, CB * q, CB) for q in range(8)]
            tiles = move_lanes(moves, 3, came, ROWS)
            grid = jnp.concatenate(tiles, axis=1)
            mixed = forced[a0 + a].astype(F32) + grid
            active = jax.nn.gelu(mixed).astype(BF16)
            result = mixed + jnp.dot(active, mix_ref[...], preferred_element_type=F32)
            result = result.astype(BF16)
            atm_out[a0 + a] = result[0:LONS]
            fluxes = lax.dot_general(
                fwt, result, (((1,), (1,)), ((), ())), preferred_element_type=F32
            )
            flux_out[a0 + a] = fluxes[0:4, 0:LONS]

    ti_copy.wait()
    zi_wait(0)
    inverse(0)
    zi_wait(1)
    inverse(1)
    xi_wait(0)
    finish(0)
    xi_wait(1)
    finish(1)

    for k in range(2):
        x_all(k, x_send, x_recv).wait_send()
        x_all(k, xi_send, xi_recv).wait_send()
        peers_all(k, z_send, z_recv, lambda copy: copy.wait_send())
    peers_all(1, zi_send, zi_recv, lambda copy: copy.wait_send())
    for copy in (lat_low, lat_high, lon_low, lon_high):
        copy.wait_send()


def local(
    atmosphere, ocean_state, surface_flux, land_sea, surface_read, surface_gain, legendre,
    spectral_gain, mixing, flux_weight, flux_embed, conv_kernel, norm_gain, ocean_up, ocean_down,
):
    forward_table, inverse_table = lon_tables()
    vm = pl.BlockSpec(memory_space=pltpu.VMEM)
    hbm = pl.BlockSpec(memory_space=pl.ANY)
    wide = [w for _, _, w in CHUNKS]

    def pair(*dims):
        return [pltpu.VMEM(dims + (w,), BF16) for w in wide]

    def message(count):
        return [pltpu.VMEM((count, 48, 384), BF16), pltpu.VMEM((count, 80, 128), BF16)]

    def crossing(*dims):
        return [pltpu.VMEM(dims + (ROWS, 384), BF16), pltpu.VMEM(dims + (288, 128), BF16)]

    dma = pltpu.SemaphoreType.DMA
    atm_next, flux_next, ocean_next = pl.pallas_call(
        body,
        out_shape=(
            jax.ShapeDtypeStruct((LATS, LONS, C), BF16),
            jax.ShapeDtypeStruct((LATS, 4, LONS), F32),
            jax.ShapeDtypeStruct((LATS, LONS, OC), BF16),
        ),
        in_specs=[vm] * 6 + [hbm] + [vm] * 8 + [hbm] * 2,
        out_specs=(vm, vm, vm),
        scratch_shapes=[
            pltpu.VMEM((2 * M, 4 * ROWS), BF16),
            pltpu.VMEM((4 * ROWS, 2 * M), BF16),
            pltpu.VMEM((LATS, C, C), BF16),
            pltpu.VMEM((LATS, C, C), BF16),
            pltpu.VMEM((LATS, C, C), BF16),
            pltpu.VMEM((LATS, ROWS, C), BF16),
            *crossing(8),
            *crossing(2, 4),
            pltpu.VMEM((2, 4 * ROWS, 256), BF16),
            *message(PEERS),
            *message(PEERS),
            pltpu.VMEM((5, 768, 128), F32),
            pltpu.VMEM((5, 768, 128), F32),
            *message(16),
            *message(PEERS),
            *pair(2, 768),
            *crossing(8),
            *crossing(8),
            pltpu.VMEM((LATS, C, 128), F32),
            pltpu.VMEM((LATS, C, 128), BF16),
            pltpu.VMEM((128, C), F32),
            pltpu.VMEM((C, 128), F32),
            pltpu.VMEM((128, 256), F32),
            pltpu.VMEM((256, 128), F32),
            pltpu.VMEM((16, C), F32),
            pltpu.VMEM((LATS + 6, ROWS, 256), BF16),
            pltpu.VMEM((LATS + 6, 16, 256), BF16),
            pltpu.VMEM((LATS + 6, 16, 256), BF16),
            pltpu.VMEM((LATS + 6, 16, 256), BF16),
            pltpu.VMEM((LATS + 6, 16, 256), BF16),
            pltpu.VMEM((LATS + 6, ROWS, 256), F32),
            pltpu.VMEM((56, 256), F32),
            dma((3,)), dma((2,)), dma((2,)), dma((2,)), dma((2,)), dma((2,)), dma((2,)),
            dma((2,)), dma((2,)), dma((4,)), dma((4,)), dma((8,)),
        ],
        compiler_params=pltpu.CompilerParams(
            collective_id=0, has_side_effects=True, vmem_limit_bytes=VMEM_LIMIT
        ),
        name="window",
    )(
        atmosphere, ocean_state,
        jnp.transpose(surface_flux, (1, 0, 2)), land_sea, surface_read,
        surface_gain.reshape(3, 128), legendre, spectral_gain.T, mixing, flux_weight.T, flux_embed,
        conv_kernel, norm_gain.reshape(1, OC), ocean_up, ocean_down.T,
        jnp.asarray(forward_table), jnp.asarray(inverse_table),
    )
    return atm_next, jnp.transpose(flux_next, (1, 0, 2)), ocean_next


def solution(mesh):
    grid = P("atm", ("ocn", "ch"), None)
    return jax.shard_map(
        local,
        mesh=mesh,
        in_specs=(
            grid, grid, P(None, "atm", ("ocn", "ch")), P("atm", ("ocn", "ch")), P(), P(),
            P("atm", None, None), P(None, ("ocn", "ch")), P(), P(), P(), P(), P(), P(), P(),
        ),
        out_specs=(grid, P(None, "atm", ("ocn", "ch")), grid),
        check_vma=False,
    )
```

```python
import math

import jax
import jax.numpy as jnp
import ml_dtypes
import numpy as np
from jax import lax
from jax.experimental import pallas as pl
from jax.experimental.pallas import tpu as pltpu
from jax.sharding import PartitionSpec as P

M = 384
NLON = 1440
C = 384
OC = 200
HID = 800
LATS = 12
LONS = 180
ROWS = 192
CB = 48
PEERS = 32
MODES = 24
CHUNKS = ((0, 8, 384), (8, 4, 256))
MESH = pl.DeviceIdType.MESH
F32 = jnp.float32
BF16 = jnp.bfloat16
VMEM_LIMIT = 60 * 2**20


def lon_tables():
    lon = np.arange(NLON, dtype=np.int64)
    wave = np.arange(M, dtype=np.int64)
    phase = (lon[:, None] * wave[None, :]) % NLON
    angle = phase.astype(np.float32) * np.float32(2.0 * math.pi / NLON)
    table = np.stack([np.cos(angle), -np.sin(angle)], axis=2) * np.float32(NLON**-0.5)
    table = table.astype(np.float32).reshape(4, 2, LONS, 2 * M).transpose(1, 0, 2, 3)
    padded = np.zeros((2, 4, ROWS, 2 * M), np.float32)
    padded[:, :, :LONS] = table
    inverse = padded.reshape(2, 4 * ROWS, 2 * M).astype(ml_dtypes.bfloat16)
    return np.ascontiguousarray(inverse.transpose(0, 2, 1)), inverse


def segments(src, dst, count):
    out = []
    done = 0
    while done < count:
        s, d = src + done, dst + done
        step = min(count - done, 128 - s % 128, 128 - d % 128)
        out.append((s // 128, d // 128, (d - s) % 128, d % 128, d % 128 + step))
        done += step
    return out


def move_lanes(moves, tiles, get, rows):
    lane = lax.broadcasted_iota(jnp.int32, (rows, 128), 1)
    out = [None] * tiles
    for key, src, dst, count in moves:
        for s_tile, d_tile, shift, low, high in segments(src, dst, count):
            piece = get(key, s_tile)
            if shift:
                piece = pltpu.roll(piece, shift, axis=1)
            if out[d_tile] is None:
                if low == 0:
                    out[d_tile] = jnp.where(lane < high, piece, 0.0)
                else:
                    out[d_tile] = jnp.where((lane >= low) & (lane < high), piece, 0.0)
            else:
                out[d_tile] = jnp.where((lane >= low) & (lane < high), piece, out[d_tile])
    return out


def body(
    atm_ref, oc_ref, flux_ref, land_ref, read_ref, gain_ref, leg_hbm, sgain_ref, mix_ref, fw_ref,
    embed_ref, ck_ref, ngain_ref, up_ref, down_ref, tf_hbm, ti_hbm,
    atm_out, flux_out, oc_out,
    tf, ti, leg, leg_p, leg_t, forced,
    pack_a, pack_b, got_a, got_b, gin, spec_a, spec_b, rspec_a, rspec_b, rsum, ssum,
    syn_a, syn_b, rsyn_a, rsyn_b, sy_a, sy_b, gs_a, gs_b, rg_a, rg_b,
    coef, filt, sgs, sg2, cols, colt, fws, drv, edge_l, edge_r, halo_l, halo_r, cpad, cker,
    in_sem, x_send, x_recv, z_send, z_recv, zi_send, zi_recv, xi_send, xi_recv, h_send, h_recv, loc_sem,
):
    pack, got, spec, rspec = (pack_a, pack_b), (got_a, got_b), (spec_a, spec_b), (rspec_a, rspec_b)
    syn, rsyn, sy, gs, rg = (syn_a, syn_b), (rsyn_a, rsyn_b), (sy_a, sy_b), (gs_a, gs_b), (rg_a, rg_b)
    a_id = lax.axis_index("atm")
    x = lax.axis_index("ocn")
    h = lax.axis_index("ch")
    core = lax.rem(a_id, 2)
    yz = a_id // 2
    y0 = yz // 4
    z0 = lax.rem(yz, 4)
    me = 2 * x + core
    lon_block = 2 * x + h
    self_peer = core == h
    n_remote = PEERS - self_peer.astype(jnp.int32)

    tf_copy = pltpu.make_async_copy(tf_hbm.at[h], tf, in_sem.at[0])
    ti_copy = pltpu.make_async_copy(ti_hbm.at[h], ti, in_sem.at[1])
    leg_copy = pltpu.make_async_copy(leg_hbm, leg, in_sem.at[2])
    tf_copy.start()
    leg_copy.start()
    ti_copy.start()

    def row_dev(q):
        return {"atm": 2 * yz + lax.rem(q, 2), "ocn": q // 2, "ch": h}

    def mode_dev(j):
        return {"atm": j, "ocn": x, "ch": core}

    def band_dev(j):
        return {"atm": (j // 2) * 2 + h, "ocn": x, "ch": lax.rem(j, 2)}

    def lat_dev(step):
        return {"atm": lax.rem(a_id + step + 32, 32), "ocn": x, "ch": h}

    def lon_dev(step):
        b = lax.rem(lon_block + step + 8, 8)
        return {"atm": a_id, "ocn": b // 2, "ch": lax.rem(b, 2)}

    barrier = pltpu.get_barrier_semaphore()

    def greet(device):
        pl.semaphore_signal(barrier, inc=1, device_id=device, device_id_type=MESH)

    def greet_row(i, carry):
        greet(row_dev(lax.rem(me + i, 8)))
        return carry

    lax.fori_loop(1, 8, greet_row, 0)
    for step in (-1, 1):
        greet(lat_dev(step))
        greet(lon_dev(step))

    def greet_peers(j, carry):
        @pl.when(jnp.logical_not(self_peer & (j == a_id)))
        def _():
            greet(mode_dev(j))

        @pl.when(jnp.logical_not(self_peer & (j == 2 * yz + h)))
        def _():
            greet(band_dev(j))

        return carry

    lax.fori_loop(0, PEERS, greet_peers, 0)

    forced[:, 176:192, :] = jnp.zeros((LATS, 16, C), BF16)

    read_row = read_ref[...].astype(F32).reshape(1, OC)

    def force(a, carry):
        seen = oc_ref[a].astype(F32) * read_row
        surface = jnp.sum(seen, axis=1, keepdims=True)
        for t in range(3):
            part = slice(128 * t, 128 * t + 128)
            total = atm_ref[a, :, part].astype(F32) + surface * gain_ref[t : t + 1, :]
            forced[a, 0:LONS, part] = total.astype(BF16)
        return carry

    lax.fori_loop(0, LATS, force, 0)

    def share(low, high):
        lanes = lax.broadcasted_iota(jnp.int32, low.shape, 1)
        return jnp.where(lanes < 64, low, pltpu.roll(high, 64, axis=1))

    def pack_chunk(k):
        a0, na, width = CHUNKS[k]

        def pieces(r0):
            held = {}
            for a in range(na):
                for t in range(3):
                    held[a, t] = forced[a0 + a, pl.ds(r0, 48), 128 * t : 128 * t + 128].astype(F32)
            for q in range(8):
                moves = [(a, CB * q, CB * a, CB) for a in range(na)]
                yield q, move_lanes(moves, width // 128, lambda key, t: held[key, t], 48)

        def whole_step(rb, carry):
            r0 = pl.multiple_of(rb * 48, 16)
            for q, tiles in pieces(r0):
                for t, value in enumerate(tiles):
                    pack[k][q, pl.ds(r0, 48), 128 * t : 128 * t + 128] = value.astype(BF16)
            return carry

        def shared_step(rb, carry):
            r0 = pl.multiple_of(rb * 48, 16)
            r1 = pl.multiple_of(rb * 48 + 96, 16)
            r2 = pl.multiple_of(rb * 48 + ROWS, 16)
            for (q, low), (_, high) in zip(pieces(r0), pieces(r1)):
                pack[k][q, pl.ds(r0, 48), :] = low[0].astype(BF16)
                pack[k][q, pl.ds(r1, 48), :] = high[0].astype(BF16)
                pack[k][q, pl.ds(r2, 48), :] = share(low[1], high[1]).astype(BF16)
            return carry

        if k == 0:
            lax.fori_loop(0, 4, whole_step, 0)
        else:
            lax.fori_loop(0, 2, shared_step, 0)

    def x_copy(k, q):
        return pltpu.make_async_remote_copy(
            src_ref=pack[k].at[q], dst_ref=got[k].at[core, x], send_sem=x_send.at[k],
            recv_sem=x_recv.at[k], device_id=row_dev(q), device_id_type=MESH,
        )

    def x_start(k):
        pltpu.make_async_copy(pack[k].at[me], got[k].at[core, x], loc_sem.at[k]).start()

        def go(i, carry):
            x_copy(k, lax.rem(me + i, 8)).start()
            return carry

        lax.fori_loop(1, 8, go, 0)

    def covers(ref, send, recv):
        return pltpu.make_async_remote_copy(
            src_ref=ref, dst_ref=ref, send_sem=send, recv_sem=recv,
            device_id=lat_dev(1), device_id_type=MESH,
        )

    def x_all(k, send, recv):
        return covers(pack[k].at[pl.ds(0, 7)], send.at[k], recv.at[k])

    def x_wait(k):
        pltpu.make_async_copy(pack[k].at[me], got[k].at[core, x], loc_sem.at[k]).wait()
        x_all(k, x_send, x_recv).wait_recv()

    pack_chunk(1)
    pl.semaphore_wait(barrier, 2 * n_remote + 7 + 4)
    x_start(1)
    pack_chunk(0)

    cols[...] = jnp.zeros_like(cols)
    for a in range(LATS):
        cols[4 * a : 4 * a + 4, 0:LONS] = flux_ref[a]
    cols[64 : 64 + LATS, 0:LONS] = land_ref[...].astype(F32)
    colt[...] = jnp.transpose(cols[...], (1, 0))
    drv[3:15, 176:192, :] = jnp.zeros((LATS, 16, 256), BF16)
    drv[3:15, :, 128:256] = jnp.zeros((LATS, ROWS, 128), BF16)
    for a in range(LATS):
        total = oc_ref[a].astype(F32)
        for f in range(4):
            total = total + colt[0:LONS, 4 * a + f : 4 * a + f + 1] * embed_ref[f : f + 1, :]
        drv[a + 3, 0:LONS, 0:OC] = total.astype(BF16)

    lat_low = pltpu.make_async_remote_copy(
        src_ref=drv.at[pl.ds(12, 3)], dst_ref=drv.at[pl.ds(0, 3)], send_sem=h_send.at[0],
        recv_sem=h_recv.at[0], device_id=lat_dev(1), device_id_type=MESH,
    )
    lat_high = pltpu.make_async_remote_copy(
        src_ref=drv.at[pl.ds(3, 3)], dst_ref=drv.at[pl.ds(15, 3)], send_sem=h_send.at[1],
        recv_sem=h_recv.at[1], device_id=lat_dev(-1), device_id_type=MESH,
    )
    lat_low.start()
    lat_high.start()

    sgs[...] = jnp.zeros_like(sgs)
    sgs[0:CB] = sgain_ref[...]
    sgs[CB : 2 * CB] = sgain_ref[...]
    sg2[...] = jnp.transpose(sgs[...], (1, 0))
    fws[...] = jnp.zeros_like(fws)
    fws[0:4] = fw_ref[...].astype(F32)
    fwt = fws[...].astype(BF16)
    cker[...] = jnp.zeros_like(cker)
    for i in range(7):
        cker[8 * i : 8 * i + 7, 0:OC] = ck_ref[i]

    slot = 2 * yz + h

    def z_copy(k, j):
        return pltpu.make_async_remote_copy(
            src_ref=spec[k].at[j], dst_ref=rspec[k].at[slot], send_sem=z_send.at[k],
            recv_sem=z_recv.at[k], device_id=mode_dev(j), device_id_type=MESH,
        )

    def z_local(k):
        return pltpu.make_async_copy(spec[k].at[a_id], rspec[k].at[slot], loc_sem.at[2 + k])

    blank = jnp.zeros((8, 128), F32)

    def forward(k):
        width = CHUNKS[k][2]
        if k == 1:
            for s in range(2):
                for n in range(4):
                    gin[s, ROWS * n : ROWS * n + ROWS, 0:128] = got[k][s, n, 0:ROWS, :]
                    tile = got[k][s, n, ROWS:288, :]
                    gin[s, ROWS * n : ROWS * n + 96, 128:256] = tile
                    turned = pltpu.roll(tile.astype(F32), 64, axis=1).astype(BF16)
                    gin[s, ROWS * n + 96 : ROWS * n + ROWS, 128:256] = turned

        def rhs(s):
            return gin[s] if k == 1 else got[k][s].reshape(4 * ROWS, width)

        def step(i, carry):
            yb = lax.rem(y0 + i, 4)
            lhs = tf[pl.ds(pl.multiple_of(yb * 192, 16), 192), :]
            halves = [
                jnp.dot(lhs, rhs(s), preferred_element_type=F32)
                for s in range(2)
            ]
            for n in range(8):
                part = slice(MODES * n, MODES * n + MODES)
                low, high = halves[0][part], halves[1][part]
                if k == 0:
                    both = jnp.concatenate([low, high], axis=0)
                else:
                    tile = share(low[:, 128:256], high[:, 128:256])
                    both = jnp.concatenate([low[:, 0:128], high[:, 0:128], tile, blank], axis=0)
                spec[k][yb * 8 + n] = both.astype(BF16)

            def send(n, c2):
                j = yb * 8 + lax.rem(2 * z0 + n, 8)
                mine = self_peer & (j == a_id)

                @pl.when(jnp.logical_not(mine))
                def _():
                    z_copy(k, j).start()

                @pl.when(mine)
                def _():
                    z_local(k).start()

                return c2

            lax.fori_loop(0, 8, send, 0)
            return carry

        lax.fori_loop(0, 4, step, 0)

    def peers_all(k, send, recv, act):
        @pl.when(self_peer)
        def _():
            act(covers(rspec[k].at[pl.ds(0, PEERS - 1)], send.at[k], recv.at[k]))

        @pl.when(jnp.logical_not(self_peer))
        def _():
            act(covers(rspec[k], send.at[k], recv.at[k]))

    tf_copy.wait()
    x_all(1, x_send, x_recv).wait_send()
    x_start(0)
    x_wait(1)
    forward(1)

    lat_low.wait_recv()
    lat_high.wait_recv()

    @pl.when(a_id == 0)
    def _():
        drv[0:3] = jnp.zeros((3, ROWS, 256), BF16)

    @pl.when(a_id == 31)
    def _():
        drv[15:18] = jnp.zeros((3, ROWS, 256), BF16)

    edge_l[...] = drv[:, 0:16, :]
    edge_r[...] = drv[:, 176:192, :]
    lon_low = pltpu.make_async_remote_copy(
        src_ref=edge_r, dst_ref=halo_l, send_sem=h_send.at[2],
        recv_sem=h_recv.at[2], device_id=lon_dev(1), device_id_type=MESH,
    )
    lon_high = pltpu.make_async_remote_copy(
        src_ref=edge_l, dst_ref=halo_r, send_sem=h_send.at[3],
        recv_sem=h_recv.at[3], device_id=lon_dev(-1), device_id_type=MESH,
    )
    lon_low.start()
    lon_high.start()

    leg_copy.wait()
    new = lax.broadcasted_iota(jnp.int32, (C, C), 0)
    old = lax.broadcasted_iota(jnp.int32, (C, C), 1)
    order = (old == lax.rem(new, 32) * LATS + new // 32).astype(F32).astype(BF16)

    def permute(m, carry):
        table = leg[m]
        leg_p[m] = lax.dot_general(
            table, order, (((1,), (1,)), ((), ())), preferred_element_type=F32
        ).astype(BF16)
        leg_t[m] = lax.dot_general(
            order, table, (((1,), (1,)), ((), ())), preferred_element_type=F32
        ).astype(BF16)
        return carry

    lax.fori_loop(0, LATS, permute, 0)

    x_wait(0)
    forward(0)

    lon_low.wait_recv()
    lon_high.wait_recv()

    def place(r, carry):
        cpad[r, 0:8, :] = pltpu.roll(halo_l[r].astype(F32), 15, axis=0)[0:8]
        cpad[r, 176:192, :] = jnp.zeros((16, 256), F32)
        cpad[r, 183:189, :] = halo_r[r].astype(F32)[0:6]
        cpad[r, 3:183, :] = drv[r, 0:LONS, :].astype(F32)
        return carry

    lax.fori_loop(0, LATS + 6, place, 0)
    lane = lax.broadcasted_iota(jnp.int32, (ROWS, 256), 1)

    def ocean(a, carry):
        halves = []
        for t in range(2):
            part = slice(128 * t, 128 * t + 128)
            total = None
            for j in range(7):
                acc = None
                for i in range(7):
                    term = cker[8 * i + j : 8 * i + j + 1, part] * cpad[a + i, :, part]
                    acc = term if acc is None else acc + term
                if j:
                    acc = pltpu.roll(acc, ROWS - j, axis=0)
                total = acc if total is None else total + acc
            halves.append(total)
        conv = jnp.concatenate(halves, axis=1)
        mean = jnp.sum(conv, axis=1, keepdims=True) * (1.0 / OC)
        centred = jnp.where(lane < OC, conv - mean, 0.0)
        var = jnp.sum(centred * centred, axis=1, keepdims=True) * (1.0 / OC)
        scaled = centred * lax.rsqrt(var + 1e-05)
        normed = (scaled[:, 0:OC] * ngain_ref[...]).astype(BF16)
        hidden = jax.nn.gelu(
            jnp.dot(normed, up_ref[...], preferred_element_type=F32)
        ).astype(BF16)
        update = lax.dot_general(
            hidden, down_ref[...], (((1,), (1,)), ((), ())), preferred_element_type=F32
        )
        mask_lane = lax.broadcasted_iota(jnp.int32, (ROWS, 128), 1)
        sea = jnp.sum(
            jnp.where(mask_lane == 64 + a, colt[0:ROWS, :], 0.0), axis=1, keepdims=True
        )
        held = drv[a + 3, :, 0:OC].astype(F32) + update
        oc_out[a] = jnp.where(sea == 1.0, held, 0.0)[0:LONS].astype(BF16)
        return carry

    lax.fori_loop(0, LATS, ocean, 0)

    def add_halves(k):

        def step(i, carry):
            both = rspec[k][2 * i].astype(F32) + rspec[k][2 * i + 1].astype(F32)
            at = pl.ds(pl.multiple_of(i * 48, 8), 48)
            if k == 0:
                for t in range(3):
                    rsum[t, at, :] = both[:, 128 * t : 128 * t + 128]
            else:
                rsum[3, at, :] = both[0:48]
                tile = both[48:72]
                rsum[4, at, :] = jnp.concatenate([tile, pltpu.roll(tile, 64, axis=1)], axis=0)
            return carry

        lax.fori_loop(0, 16, step, 0)

    def z_wait(k):
        peers_all(k, z_send, z_recv, lambda copy: copy.wait_recv())

        @pl.when(self_peer)
        def _():
            z_local(k).wait()

    spans = ((range(0, 8), 0, 3), (range(8, LATS), 3, 5))

    def gather(k, m):
        bands, first, end = spans[k]
        rows = {
            (p, t): rsum[t, pl.ds(2 * m + p, 32, stride=MODES), :]
            for p in range(2)
            for t in range(first, end)
        }
        blocks = []
        for a in bands:
            moves = [(p, CB * a, CB * p, CB) for p in range(2)]
            blocks.append(move_lanes(moves, 1, lambda key, t: rows[key, t], 32)[0])
        return jnp.concatenate(blocks, axis=0).astype(BF16)

    def scatter(k, m, synth):
        bands, first, end = spans[k]
        for p in range(2):
            moves = [(n, CB * p, CB * a - 128 * first, CB) for n, a in enumerate(bands)]
            tiles = move_lanes(
                moves, end - first, lambda key, t: synth[32 * key : 32 * key + 32], 32
            )
            for t, value in enumerate(tiles):
                ssum[first + t, pl.ds(2 * m + p, 32, stride=MODES), :] = value

    def each_mode(work):
        def go(i, carry):
            for n in range(3):
                work(3 * i + n)
            return carry

        lax.fori_loop(0, LATS // 3, go, 0)

    def early(m):
        coef[m] = jnp.dot(leg_p[m, :, 256:384], gather(1, m), preferred_element_type=F32)

    def middle(m):
        coeffs = coef[m] + jnp.dot(leg_p[m, :, 0:256], gather(0, m), preferred_element_type=F32)
        filtered = (coeffs * sg2[...]).astype(BF16)
        filt[m] = filtered
        scatter(0, m, jnp.dot(leg_t[m, 0:256, :], filtered, preferred_element_type=F32))

    def late(m):
        scatter(1, m, jnp.dot(leg_t[m, 256:384, :], filt[m], preferred_element_type=F32))

    z_wait(1)
    add_halves(1)
    each_mode(early)
    z_wait(0)
    add_halves(0)
    each_mode(middle)

    def zi_copy(k, j):
        return pltpu.make_async_remote_copy(
            src_ref=syn[k].at[j // 2], dst_ref=rsyn[k].at[a_id], send_sem=zi_send.at[k],
            recv_sem=zi_recv.at[k], device_id=band_dev(j), device_id_type=MESH,
        )

    def zi_local(k):
        return pltpu.make_async_copy(syn[k].at[yz], rsyn[k].at[a_id], loc_sem.at[4 + k])

    def back(k, fill, send):
        def step(i, carry):
            b = lax.rem(y0 + i // 4, 4) * 4 + lax.rem(z0 + i, 4)
            at = pl.ds(pl.multiple_of(b * 48, 8), 48)
            if fill and k == 0:
                for t in range(3):
                    syn[k][b, :, 128 * t : 128 * t + 128] = ssum[t, at, :].astype(BF16)
            elif fill:
                last = ssum[4, at, :]
                tile = share(last[0:MODES], last[MODES:48])
                both = jnp.concatenate([ssum[3, at, :], tile, blank], axis=0)
                syn[k][b] = both.astype(BF16)
            for n in range(2 if send else 0):
                j = 2 * b + n
                mine = self_peer & (j == 2 * yz + h)

                @pl.when(jnp.logical_not(mine))
                def _():
                    zi_copy(k, j).start()

                @pl.when(mine)
                def _():
                    zi_local(k).start()

            return carry

        lax.fori_loop(0, 16, step, 0)

    back(0, True, True)
    each_mode(late)
    back(1, True, False)
    peers_all(0, zi_send, zi_recv, lambda copy: copy.wait_send())
    back(1, False, True)

    def zi_wait(k):
        peers_all(k, zi_send, zi_recv, lambda copy: copy.wait_recv())

        @pl.when(self_peer)
        def _():
            zi_local(k).wait()

    def xi_copy(k, q):
        return pltpu.make_async_remote_copy(
            src_ref=gs[k].at[q], dst_ref=rg[k].at[me], send_sem=xi_send.at[k],
            recv_sem=xi_recv.at[k], device_id=row_dev(q), device_id_type=MESH,
        )

    def xi_local(k):
        return pltpu.make_async_copy(gs[k].at[me], rg[k].at[me], loc_sem.at[6 + k])

    def inverse(k):
        def regroup(i, carry):
            first = rsyn[k][2 * i].astype(F32)
            second = rsyn[k][2 * i + 1].astype(F32)
            for s in range(2):
                part = slice(MODES * s, MODES * s + MODES)
                at = pl.ds(pl.multiple_of(i * 48, 16), 48)
                both = jnp.concatenate([first[part], second[part]], axis=0)
                if k == 0:
                    sy[k][s, at, :] = both.astype(BF16)
                else:
                    sy[k][s, at, 0:128] = both.astype(BF16)
                    both = jnp.concatenate([first[48:72], second[48:72]], axis=0)
                    if s:
                        both = pltpu.roll(both, 64, axis=1)
                    sy[k][s, at, 128:256] = both.astype(BF16)
            return carry

        lax.fori_loop(0, 16, regroup, 0)

        def step(i, carry):
            xb = lax.rem(x + i, 4)
            lhs = ti[pl.ds(pl.multiple_of(xb * ROWS, 16), ROWS), :]
            for s in range(2):
                q = 2 * xb + s
                values = jnp.dot(lhs, sy[k][s], preferred_element_type=F32)
                if k == 1:
                    tile = share(values[0:96, 128:256], values[96:ROWS, 128:256])
                    values = jnp.concatenate([values[:, 0:128], tile], axis=0)
                gs[k][q] = values.astype(BF16)

                @pl.when(q != me)
                def _():
                    xi_copy(k, q).start()

                @pl.when(q == me)
                def _():
                    xi_local(k).start()

            return carry

        lax.fori_loop(0, 4, step, 0)

    def xi_wait(k):
        x_all(k, xi_send, xi_recv).wait_recv()
        xi_local(k).wait()

    def finish(k):
        a0, na, width = CHUNKS[k]

        def came(q, t):
            if k == 0:
                return rg[k][q, :, 128 * t : 128 * t + 128].astype(F32)
            if t == 0:
                return rg[k][q, 0:ROWS, :].astype(F32)
            tile = rg[k][q, ROWS:288, :].astype(F32)
            return jnp.concatenate([tile, pltpu.roll(tile, 64, axis=1)], axis=0)

        for a in range(na):
            moves = [(q, CB * a, CB * q, CB) for q in range(8)]
            tiles = move_lanes(moves, 3, came, ROWS)
            grid = jnp.concatenate(tiles, axis=1)
            mixed = forced[a0 + a].astype(F32) + grid
            active = jax.nn.gelu(mixed).astype(BF16)
            result = mixed + jnp.dot(active, mix_ref[...], preferred_element_type=F32)
            result = result.astype(BF16)
            atm_out[a0 + a] = result[0:LONS]
            fluxes = lax.dot_general(
                fwt, result, (((1,), (1,)), ((), ())), preferred_element_type=F32
            )
            flux_out[a0 + a] = fluxes[0:4, 0:LONS]

    ti_copy.wait()
    zi_wait(0)
    inverse(0)
    zi_wait(1)
    inverse(1)
    xi_wait(0)
    finish(0)
    xi_wait(1)
    finish(1)

    x_all(0, x_send, x_recv).wait_send()
    for k in range(2):
        x_all(k, xi_send, xi_recv).wait_send()
        peers_all(k, z_send, z_recv, lambda copy: copy.wait_send())
    peers_all(1, zi_send, zi_recv, lambda copy: copy.wait_send())
    for copy in (lat_low, lat_high, lon_low, lon_high):
        copy.wait_send()


def local(
    atmosphere, ocean_state, surface_flux, land_sea, surface_read, surface_gain, legendre,
    spectral_gain, mixing, flux_weight, flux_embed, conv_kernel, norm_gain, ocean_up, ocean_down,
):
    forward_table, inverse_table = lon_tables()
    vm = pl.BlockSpec(memory_space=pltpu.VMEM)
    hbm = pl.BlockSpec(memory_space=pl.ANY)
    wide = [w for _, _, w in CHUNKS]

    def pair(*dims):
        return [pltpu.VMEM(dims + (w,), BF16) for w in wide]

    def message(count):
        return [pltpu.VMEM((count, 48, 384), BF16), pltpu.VMEM((count, 80, 128), BF16)]

    def crossing(*dims):
        return [pltpu.VMEM(dims + (ROWS, 384), BF16), pltpu.VMEM(dims + (288, 128), BF16)]

    dma = pltpu.SemaphoreType.DMA
    atm_next, flux_next, ocean_next = pl.pallas_call(
        body,
        out_shape=(
            jax.ShapeDtypeStruct((LATS, LONS, C), BF16),
            jax.ShapeDtypeStruct((LATS, 4, LONS), F32),
            jax.ShapeDtypeStruct((LATS, LONS, OC), BF16),
        ),
        in_specs=[vm] * 6 + [hbm] + [vm] * 8 + [hbm] * 2,
        out_specs=(vm, vm, vm),
        scratch_shapes=[
            pltpu.VMEM((2 * M, 4 * ROWS), BF16),
            pltpu.VMEM((4 * ROWS, 2 * M), BF16),
            pltpu.VMEM((LATS, C, C), BF16),
            pltpu.VMEM((LATS, C, C), BF16),
            pltpu.VMEM((LATS, C, C), BF16),
            pltpu.VMEM((LATS, ROWS, C), BF16),
            *crossing(8),
            *crossing(2, 4),
            pltpu.VMEM((2, 4 * ROWS, 256), BF16),
            *message(PEERS),
            *message(PEERS),
            pltpu.VMEM((5, 768, 128), F32),
            pltpu.VMEM((5, 768, 128), F32),
            *message(16),
            *message(PEERS),
            *pair(2, 768),
            *crossing(8),
            *crossing(8),
            pltpu.VMEM((LATS, C, 128), F32),
            pltpu.VMEM((LATS, C, 128), BF16),
            pltpu.VMEM((128, C), F32),
            pltpu.VMEM((C, 128), F32),
            pltpu.VMEM((128, 256), F32),
            pltpu.VMEM((256, 128), F32),
            pltpu.VMEM((16, C), F32),
            pltpu.VMEM((LATS + 6, ROWS, 256), BF16),
            pltpu.VMEM((LATS + 6, 16, 256), BF16),
            pltpu.VMEM((LATS + 6, 16, 256), BF16),
            pltpu.VMEM((LATS + 6, 16, 256), BF16),
            pltpu.VMEM((LATS + 6, 16, 256), BF16),
            pltpu.VMEM((LATS + 6, ROWS, 256), F32),
            pltpu.VMEM((56, 256), F32),
            dma((3,)), dma((2,)), dma((2,)), dma((2,)), dma((2,)), dma((2,)), dma((2,)),
            dma((2,)), dma((2,)), dma((4,)), dma((4,)), dma((8,)),
        ],
        compiler_params=pltpu.CompilerParams(
            collective_id=0, has_side_effects=True, vmem_limit_bytes=VMEM_LIMIT
        ),
        name="window",
    )(
        atmosphere, ocean_state,
        jnp.transpose(surface_flux, (1, 0, 2)), land_sea, surface_read,
        surface_gain.reshape(3, 128), legendre, spectral_gain.T, mixing, flux_weight.T, flux_embed,
        conv_kernel, norm_gain.reshape(1, OC), ocean_up, ocean_down.T,
        jnp.asarray(forward_table), jnp.asarray(inverse_table),
    )
    return atm_next, jnp.transpose(flux_next, (1, 0, 2)), ocean_next


def solution(mesh):
    grid = P("atm", ("ocn", "ch"), None)
    return jax.shard_map(
        local,
        mesh=mesh,
        in_specs=(
            grid, grid, P(None, "atm", ("ocn", "ch")), P("atm", ("ocn", "ch")), P(), P(),
            P("atm", None, None), P(None, ("ocn", "ch")), P(), P(), P(), P(), P(), P(), P(),
        ),
        out_specs=(grid, P(None, "atm", ("ocn", "ch")), grid),
        check_vma=False,
    )
```
